128 devices in a mesh: row: 8 (over x, core), col: 16 (over y, z).
Axes of the slice: x: 4, y: 4, z: 4, core: 2. Of those that a mesh axis runs over, the one named last changes fastest.
Arguments:
- child_block: bfloat16 [8, 4096, 4096], P('row', None, 'col'), may hold values from -6 to 6
- left_gen: bfloat16 [8, 4096, 512], P('row', 'col'), may hold values from -0.25 to 0.25
- core_gen: bfloat16 [8, 512, 512], P('row'), may hold values from -0.25 to 0.25
- right_gen: bfloat16 [8, 512, 4096], P('row', None, 'col'), may hold values from -6 to 6
- child_maps: int32 [8, 4096], replicated, may hold values from 0 to 8191, as said below
- parent_entries: bfloat16 [8192, 8192], P('row', 'col'), may hold values from -6 to 6
- pivot_inverse: float32 [512, 512], replicated, may hold values from -0.01171875 to 0.01171875
Outputs:
- front: float32 [8192, 8192], P('row', 'col')
The draws below stay inside these ranges and needn't reach their ends.
Inputs may be any that keep to these rules, and one draw needn't show every extreme that they name: `child_maps`: each row lists 4096 distinct parent indices. Within every aligned block of 256 positions of a row, at most 24 indices fall in any one of the 16 ranges of 512 consecutive parent indices, and some block of every row reaches it; within a whole row at most 768 fall in any one of the 8 ranges of 1024 consecutive parent indices, and every row reaches it in some range.
All inputs are finite; a program needn't handle non-finite values.
Results may differ from the reference program's by a relative error of at most 0.0047.
Values may be sent and summed in bfloat16 or wider, within the bound.
A program may use at most 128 MiB of HBM per device.

```python
import jax
import jax.numpy as jnp
from jax import lax

M = 4096
K = 512
F = 8192
W = 512
CHILDREN = 8
M_SHARD = 256
UNIT = 4
FC = 512
N_ROW = 8
N_COL = 16


def shuffled_range(sub_key, length):
    return jax.random.permutation(sub_key, length).astype(jnp.int32)


def draw_child_maps(key, part):
    key = jax.random.fold_in(key, 11)
    first_tab = jnp.array([6, 6, 4, 3], jnp.int32)
    second_tab = jnp.array([6, 2, 4, 1], jnp.int32)

    def one_child(child_key):
        owner_key, swap_key, place_key, value_key = jax.random.split(child_key, 4)
        owner = shuffled_range(owner_key, N_ROW)
        pair_ids = jnp.arange(N_ROW, dtype=jnp.int32) % 4
        first = first_tab[pair_ids] * UNIT
        second = second_tab[pair_ids] * UNIT
        flips = jax.random.randint(swap_key, (N_COL, N_ROW), 0, 2).astype(jnp.int32)
        left_count = jnp.where(flips == 1, second[None, :], first[None, :])
        right_count = (first + second)[None, :] - left_count
        counts = jnp.zeros((N_COL, N_COL), jnp.int32)
        counts = counts.at[:, 2 * owner].set(left_count)
        counts = counts.at[:, 2 * owner + 1].set(right_count)
        ends = jnp.cumsum(counts, axis=1).astype(jnp.int32)
        slots = jnp.arange(M_SHARD, dtype=jnp.int32)
        block = jnp.sum((ends[:, None, :] <= slots[None, :, None]).astype(jnp.int32), axis=2)
        starts = ends - counts
        rank = slots[None, :] - jnp.take_along_axis(starts, block, axis=1)
        before = (jnp.cumsum(counts, axis=0) - counts).astype(jnp.int32)
        offset = jnp.take_along_axis(before, block, axis=1) + rank
        orders = jax.vmap(lambda sub_key: shuffled_range(sub_key, FC))(jax.random.split(value_key, N_COL))
        values = block * FC + orders[block, offset]
        shuffles = jax.vmap(lambda sub_key: shuffled_range(sub_key, M_SHARD))(jax.random.split(place_key, N_COL))
        placed = jnp.zeros((N_COL, M_SHARD), jnp.int32)
        placed = placed.at[jnp.arange(N_COL, dtype=jnp.int32)[:, None], shuffles].set(values)
        return placed.reshape(M)
    return jax.vmap(one_child)(jax.random.split(key, CHILDREN)).astype(jnp.int32)


def block_levels(rng, extent, pieces, low, high):
    factor_of = 1.0
    for position, shards_of in pieces:
        steps = jax.random.uniform(jax.random.fold_in(jax.random.fold_in(rng, 6), position), (shards_of,), jnp.float32, low / len(pieces), high / len(pieces))
        factor_of = factor_of * jnp.repeat(jnp.exp(steps), extent[position] // shards_of).reshape((-1,) + (1,) * (len(extent) - 1 - position))
    return factor_of


def centred(rng, dims, spread, most, cuts=(), kind=jnp.bfloat16):
    level = block_levels(rng, dims, cuts, -0.22, 0.18) if cuts else 1.0
    drawn = jax.random.normal(rng, dims, jnp.float32) * spread * level
    return jnp.minimum(jnp.maximum(drawn, -most), most).astype(kind)


def setup_inputs(seed: int = 0) -> dict:
    arg_keys = jax.random.split(jax.random.key(seed), 8)
    child_block = centred(arg_keys[0], (CHILDREN, M, M), 1.0, 6.0, ((0, 8), (2, 16)))
    left_gen = centred(arg_keys[1], (CHILDREN, M, K), K ** -0.5, 0.25, ((0, 8), (1, 16)))
    core_gen = centred(arg_keys[2], (CHILDREN, K, K), K ** -0.5, 0.25, ((0, 8),))
    right_gen = centred(arg_keys[3], (CHILDREN, K, M), 1.0, 6.0, ((0, 8), (2, 16)))
    child_maps = draw_child_maps(jax.random.fold_in(arg_keys[7], 71), 0)
    parent_entries = centred(arg_keys[5], (F, F), 1.0, 6.0, ((0, 8), (1, 16)))
    pivot_inverse = centred(arg_keys[6], (W, W), (W * W) ** -0.5, 0.01171875, (), jnp.float32)
    return {"child_block": child_block, "left_gen": left_gen, "core_gen": core_gen, "right_gen": right_gen, "child_maps": child_maps, "parent_entries": parent_entries, "pivot_inverse": pivot_inverse}


def reference(child_block, left_gen, core_gen, right_gen, child_maps, parent_entries, pivot_inverse):
    assembled = parent_entries.astype(jnp.float32)
    for child in range(CHILDREN):
        mixing = jnp.dot(core_gen[child], right_gen[child], preferred_element_type=jnp.float32).astype(jnp.bfloat16)
        update = (child_block[child].astype(jnp.float32) - jnp.dot(left_gen[child], mixing, preferred_element_type=jnp.float32)).astype(jnp.bfloat16)
        index = child_maps[child].astype(jnp.int32)
        assembled = assembled.at[index[:, None], index[None, :]].add(update.astype(jnp.float32))
    panel = jnp.dot(assembled[:, :W], pivot_inverse, precision=lax.Precision.HIGHEST, preferred_element_type=jnp.float32)
    pivot = assembled[:W, W:]
    trailing = assembled[W:, W:] - jnp.dot(panel[W:], pivot, precision=lax.Precision.HIGHEST, preferred_element_type=jnp.float32)
    front = assembled.at[W:, W:].set(trailing)
    front = front.at[W:, :W].set(panel[W:])
    return front
```

```python
import jax
import jax.numpy as jnp
from jax import lax
from jax.sharding import PartitionSpec as P

BF = jnp.bfloat16
F32 = jnp.float32
HI = lax.Precision.HIGHEST


def block_slots(mask, tri):
    ranks = jnp.dot(mask.astype(BF), tri, preferred_element_type=F32).astype(jnp.int32)
    return jnp.where(mask, ranks, -1)


def slot_targets(slots, targets, count):
    hit = slots[..., None, :] == jnp.arange(count, dtype=jnp.int32)[:, None]
    return jnp.sum(jnp.where(hit, targets[..., None, :] + 1, 0), axis=-1) - 1


def bcast(value, axis, source):
    kept = jnp.where(lax.axis_index(axis) == source, value, 0).astype(value.dtype)
    return lax.psum(kept, axis)


def on_device(
    child_block, left_gen, core_gen, right_gen, child_maps, parent_entries, pivot_inverse
):
    nr = lax.axis_size("row")
    nc = lax.axis_size("col")
    row_me = lax.axis_index("row")
    col_me = lax.axis_index("col")
    order = child_block.shape[1]
    width = child_block.shape[2]
    fr, fc = parent_entries.shape
    unit = order // (16 * nr * nr)
    cs = 6 * unit
    rs = 12 * unit
    pw = pivot_inverse.shape[0]
    nb = order // width

    left = lax.all_gather(left_gen[0], "col", axis=0, tiled=True)
    mixing = jnp.dot(core_gen[0], right_gen[0], preferred_element_type=F32).astype(BF)

    blocks = child_maps.reshape(nr, nb, width)
    pos = jnp.arange(width, dtype=jnp.int32)
    tri = (pos[:, None] < pos[None, :]).astype(BF)
    mine = lax.dynamic_index_in_dim(blocks, row_me, 0, keepdims=False)
    my_cols = lax.dynamic_index_in_dim(mine, col_me, 0, keepdims=False)
    cmask = (my_cols // fc)[None, :] == jnp.arange(nc, dtype=jnp.int32)[:, None]
    cslot = block_slots(cmask, tri)
    pick_cols = (cslot[:, None, :] == jnp.arange(cs, dtype=jnp.int32)[None, :, None]).astype(BF)
    pick_cols = pick_cols.reshape(nc * cs, width)
    rmask = (mine // fr)[:, None, :] == jnp.arange(nr, dtype=jnp.int32)[None, :, None]
    rslot = block_slots(rmask, tri)
    pick_rows = (rslot[:, :, None, :] == jnp.arange(rs, dtype=jnp.int32)[None, None, :, None]).astype(BF)
    pick_rows = pick_rows.reshape(nb, nr * rs, width)
    rmask2 = (blocks // fr) == row_me
    rtarget = slot_targets(block_slots(rmask2, tri), blocks - row_me * fr, rs).reshape(nr * nb * rs)
    place_rows = (rtarget[None, :] == jnp.arange(fr, dtype=jnp.int32)[:, None]).astype(BF)
    cmask2 = (blocks // fc) == col_me
    ctarget = slot_targets(block_slots(cmask2, tri), blocks - col_me * fc, cs).reshape(nr, nb * cs)
    place_cols = (ctarget[:, :, None] == jnp.arange(fc, dtype=jnp.int32)[None, None, :]).astype(BF)

    product = jnp.dot(left, mixing, preferred_element_type=F32)
    update = (child_block[0].astype(F32) - product).astype(BF)

    sent = lax.dot_general(pick_cols, update, (((1,), (1,)), ((), ())), preferred_element_type=F32)
    sent = sent.astype(BF).reshape(nc, cs, order)
    got = lax.all_to_all(sent, "col", split_axis=0, concat_axis=0, tiled=True)
    got = got.reshape(nc * cs, nb, width)
    rows = jnp.einsum("isp,cip->isc", pick_rows, got, preferred_element_type=F32).astype(BF)
    rows = rows.reshape(nb, nr, rs, nc * cs).transpose(1, 0, 2, 3)
    moved = lax.all_to_all(rows, "row", split_axis=0, concat_axis=0, tiled=True)
    moved = moved.reshape(nr, nb * rs, nc * cs)
    wide = jnp.einsum("nsc,ncf->nsf", moved, place_cols, preferred_element_type=F32).astype(BF)
    placed = jnp.dot(place_rows, wide.reshape(nr * nb * rs, fc), preferred_element_type=F32)
    assembled = parent_entries.astype(F32) + placed

    local_panel = lax.cond(
        col_me == 0,
        lambda: jnp.dot(assembled, pivot_inverse, precision=HI, preferred_element_type=F32),
        lambda: jnp.zeros((fr, pw), F32),
    )
    panel_rows = bcast(local_panel.astype(BF), "col", 0)
    pivot = bcast(assembled[:pw, :].astype(BF), "row", 0)
    trailing = assembled - jnp.dot(panel_rows, pivot, preferred_element_type=F32)
    global_rows = row_me * fr + jnp.arange(fr, dtype=jnp.int32)
    lower = jnp.where(col_me == 0, local_panel, trailing)
    return jnp.where(global_rows[:, None] < pw, assembled, lower)


def solution(mesh):
    return jax.shard_map(
        on_device,
        mesh=mesh,
        in_specs=(
            P("row", None, "col"),
            P("row", "col", None),
            P("row", None, None),
            P("row", None, "col"),
            P(),
            P("row", "col"),
            P(),
        ),
        out_specs=P("row", "col"),
        check_vma=False,
    )
```

```python
import jax
import jax.numpy as jnp
from jax import lax
from jax.experimental import pallas as pl
from jax.experimental.pallas import tpu as pltpu
from jax.sharding import PartitionSpec as P

BF = jnp.bfloat16
F32 = jnp.float32
HI = lax.Precision.HIGHEST


def block_slots(mask, tri):
    ranks = jnp.dot(mask.astype(BF), tri, preferred_element_type=F32).astype(jnp.int32)
    return jnp.where(mask, ranks, -1)


def slot_targets(slots, targets, count):
    hit = slots[..., None, :] == jnp.arange(count, dtype=jnp.int32)[:, None]
    return jnp.sum(jnp.where(hit, targets[..., None, :] + 1, 0), axis=-1) - 1


def col_peer(me, d):
    y = lax.rem(me // 4 + d // 4, 4)
    z = lax.rem(lax.rem(me, 4) + lax.rem(d, 4), 4)
    return y * 4 + z


def row_peer(me, d):
    x = lax.rem(me // 2 + d // 2, 4)
    core = lax.rem(lax.rem(me, 2) + lax.rem(d, 2), 2)
    return x * 2 + core


def col_from(me, d):
    y = lax.rem(me // 4 + 4 - d // 4, 4)
    z = lax.rem(lax.rem(me, 4) + 4 - lax.rem(d, 4), 4)
    return y * 4 + z


def row_from(me, d):
    x = lax.rem(me // 2 + 4 - d // 2, 4)
    core = lax.rem(lax.rem(me, 2) + lax.rem(d, 2), 2)
    return x * 2 + core


def each(low, high, body):
    def step(i, carry):
        body(i)
        return carry

    lax.fori_loop(low, high, step, 0)


def greet(nr, nc, row, col):
    barrier = pltpu.get_barrier_semaphore()
    each(1, nc, lambda d: pl.semaphore_signal(
        barrier, inc=1, device_id={"col": col_peer(col, d)}, device_id_type=pl.DeviceIdType.MESH))
    each(1, nr, lambda d: pl.semaphore_signal(
        barrier, inc=1, device_id={"row": row_peer(row, d)}, device_id_type=pl.DeviceIdType.MESH))
    pl.semaphore_wait(barrier, nc + nr - 2)


def share_kernel(nr, nc, asm, pinv, panel, pivot, chunk, ss1, rs1, ss2, rs2, ss3, rs3, ss4, rs4):
    row = lax.axis_index("row")
    col = lax.axis_index("col")
    mesh = pl.DeviceIdType.MESH
    pc = panel.shape[0] // nc
    vc = pivot.shape[0] // nr

    def rows_of(ref, index, size):
        return ref.at[pl.ds(pl.multiple_of(index * size, size), size)]

    def pivot_out(d):
        return pltpu.make_async_remote_copy(
            rows_of(asm, d, vc), rows_of(pivot, d, vc), ss1.at[d], rs1.at[0],
            device_id={"row": d}, device_id_type=mesh)

    def panel_out(d):
        return pltpu.make_async_remote_copy(
            rows_of(asm, d, pc), chunk, ss2.at[d], rs2.at[0],
            device_id={"col": d}, device_id_type=mesh)

    def pivot_share(d, whose):
        part = rows_of(pivot, whose, vc)
        return pltpu.make_async_remote_copy(
            part, part, ss3.at[d], rs3.at[d],
            device_id={"row": row_peer(row, d)}, device_id_type=mesh)

    def panel_share(d, whose):
        part = rows_of(panel, whose, pc)
        return pltpu.make_async_remote_copy(
            part, part, ss4.at[d], rs4.at[d],
            device_id={"col": col_peer(col, d)}, device_id_type=mesh)

    greet(nr, nc, row, col)

    @pl.when(col == 0)
    def _():
        each(1, nc, lambda d: panel_out(d).start())
        chunk[...] = asm[0:pc, :]

    @pl.when(row == 0)
    def _():
        each(1, nr, lambda d: pivot_out(d).start())
        pivot[0:vc, :] = asm[0:vc, :]

    @pl.when(row > 0)
    def _():
        pivot_out(row).wait_recv()

    each(1, nr, lambda d: pivot_share(d, row).start())

    @pl.when(col > 0)
    def _():
        panel_out(col).wait_recv()

    part = jnp.dot(chunk[...].astype(F32), pinv[...], precision=HI, preferred_element_type=F32)
    panel[pl.ds(pl.multiple_of(col * pc, pc), pc), :] = part.astype(BF)
    each(1, nc, lambda d: panel_share(d, col).start())

    each(1, nr, lambda d: pivot_share(d, row_from(row, d)).wait_recv())
    each(1, nc, lambda d: panel_share(d, col_from(col, d)).wait_recv())
    each(1, nr, lambda d: pivot_share(d, row).wait_send())
    each(1, nc, lambda d: panel_share(d, col).wait_send())

    @pl.when(col == 0)
    def _():
        each(1, nc, lambda d: panel_out(d).wait_send())

    @pl.when(row == 0)
    def _():
        each(1, nr, lambda d: pivot_out(d).wait_send())


def share(nr, nc, asm, pinv):
    rows, cols = asm.shape
    vmem = pl.BlockSpec(memory_space=pltpu.VMEM)
    dma = pltpu.SemaphoreType.DMA
    pw = pinv.shape[0]
    return pl.pallas_call(
        lambda *refs: share_kernel(nr, nc, *refs),
        out_shape=(
            jax.ShapeDtypeStruct((rows, pw), BF),
            jax.ShapeDtypeStruct((pw, cols), BF),
        ),
        in_specs=[vmem, vmem],
        out_specs=(vmem, vmem),
        scratch_shapes=[
            pltpu.VMEM((rows // nc, pw), BF),
            dma((nr,)), dma((1,)), dma((nc,)), dma((1,)),
            dma((nr,)), dma((nr,)), dma((nc,)), dma((nc,)),
        ],
        compiler_params=pltpu.CompilerParams(
            collective_id=0, has_side_effects=True, vmem_limit_bytes=32 * 1024 * 1024
        ),
        name="share",
    )(asm, pinv)


def on_device(
    child_block, left_gen, core_gen, right_gen, child_maps, parent_entries, pivot_inverse
):
    nr = lax.axis_size("row")
    nc = lax.axis_size("col")
    row_me = lax.axis_index("row")
    col_me = lax.axis_index("col")
    order = child_block.shape[1]
    width = child_block.shape[2]
    fr, fc = parent_entries.shape
    unit = order // (16 * nr * nr)
    cs = 6 * unit
    rs = 12 * unit
    pw = pivot_inverse.shape[0]
    nb = order // width

    left = lax.all_gather(left_gen[0], "col", axis=0, tiled=True)
    mixing = jnp.dot(core_gen[0], right_gen[0], preferred_element_type=F32).astype(BF)

    blocks = child_maps.reshape(nr, nb, width)
    pos = jnp.arange(width, dtype=jnp.int32)
    tri = (pos[:, None] < pos[None, :]).astype(BF)
    mine = lax.dynamic_index_in_dim(blocks, row_me, 0, keepdims=False)
    my_cols = lax.dynamic_index_in_dim(mine, col_me, 0, keepdims=False)
    cmask = (my_cols // fc)[None, :] == jnp.arange(nc, dtype=jnp.int32)[:, None]
    cslot = block_slots(cmask, tri)
    pick_cols = (cslot[:, None, :] == jnp.arange(cs, dtype=jnp.int32)[None, :, None]).astype(BF)
    pick_cols = pick_cols.reshape(nc * cs, width)
    rmask = (mine // fr)[:, None, :] == jnp.arange(nr, dtype=jnp.int32)[None, :, None]
    rslot = block_slots(rmask, tri)
    pick_rows = (rslot[:, :, None, :] == jnp.arange(rs, dtype=jnp.int32)[None, None, :, None]).astype(BF)
    pick_rows = pick_rows.reshape(nb, nr * rs, width)
    rmask2 = (blocks // fr) == row_me
    rtarget = slot_targets(block_slots(rmask2, tri), blocks - row_me * fr, rs).reshape(nr * nb * rs)
    place_rows = (rtarget[None, :] == jnp.arange(fr, dtype=jnp.int32)[:, None]).astype(BF)
    cmask2 = (blocks // fc) == col_me
    ctarget = slot_targets(block_slots(cmask2, tri), blocks - col_me * fc, cs).reshape(nr, nb * cs)
    place_cols = (ctarget[:, :, None] == jnp.arange(fc, dtype=jnp.int32)[None, None, :]).astype(BF)

    product = jnp.dot(left, mixing, preferred_element_type=F32)
    update = (child_block[0].astype(F32) - product).astype(BF)

    sent = lax.dot_general(pick_cols, update, (((1,), (1,)), ((), ())), preferred_element_type=F32)
    sent = sent.astype(BF).reshape(nc, cs, order)
    got = lax.all_to_all(sent, "col", split_axis=0, concat_axis=0, tiled=True)
    got = got.reshape(nc * cs, nb, width)
    rows = jnp.einsum("isp,cip->isc", pick_rows, got, preferred_element_type=F32).astype(BF)
    rows = rows.reshape(nb, nr, rs, nc * cs).transpose(1, 0, 2, 3)
    moved = lax.all_to_all(rows, "row", split_axis=0, concat_axis=0, tiled=True)
    moved = moved.reshape(nr, nb * rs, nc * cs)
    wide = jnp.einsum("nsc,ncf->nsf", moved, place_cols, preferred_element_type=F32).astype(BF)
    placed = jnp.dot(place_rows, wide.reshape(nr * nb * rs, fc), preferred_element_type=F32)
    assembled = parent_entries.astype(F32) + placed

    panel_rows, pivot = share(nr, nc, assembled.astype(BF), pivot_inverse)
    local_panel = lax.cond(
        col_me == 0,
        lambda: jnp.dot(assembled, pivot_inverse, precision=HI, preferred_element_type=F32),
        lambda: jnp.zeros((fr, pw), F32),
    )
    trailing = assembled - jnp.dot(panel_rows, pivot, preferred_element_type=F32)
    global_rows = row_me * fr + jnp.arange(fr, dtype=jnp.int32)
    lower = jnp.where(col_me == 0, local_panel, trailing)
    return jnp.where(global_rows[:, None] < pw, assembled, lower)


def solution(mesh):
    return jax.shard_map(
        on_device,
        mesh=mesh,
        in_specs=(
            P("row", None, "col"),
            P("row", "col", None),
            P("row", None, None),
            P("row", None, "col"),
            P(),
            P("row", "col"),
            P(),
        ),
        out_specs=P("row", "col"),
        check_vma=False,
    )
```

```python
import jax
import jax.numpy as jnp
from jax import lax
from jax.experimental import pallas as pl
from jax.experimental.pallas import tpu as pltpu
from jax.sharding import PartitionSpec as P

BF = jnp.bfloat16
F32 = jnp.float32
HI = lax.Precision.HIGHEST


def block_slots(mask, tri):
    ranks = jnp.dot(mask.astype(BF), tri, preferred_element_type=F32).astype(jnp.int32)
    return jnp.where(mask, ranks, -1)


def slot_targets(slots, targets, count):
    hit = slots[..., None, :] == jnp.arange(count, dtype=jnp.int32)[:, None]
    return jnp.sum(jnp.where(hit, targets[..., None, :] + 1, 0), axis=-1) - 1


def col_peer(me, d):
    y = lax.rem(me // 4 + d // 4, 4)
    z = lax.rem(lax.rem(me, 4) + lax.rem(d, 4), 4)
    return y * 4 + z


def row_peer(me, d):
    x = lax.rem(me // 2 + d // 2, 4)
    core = lax.rem(lax.rem(me, 2) + lax.rem(d, 2), 2)
    return x * 2 + core


def col_from(me, d):
    y = lax.rem(me // 4 + 4 - d // 4, 4)
    z = lax.rem(lax.rem(me, 4) + 4 - lax.rem(d, 4), 4)
    return y * 4 + z


def row_from(me, d):
    x = lax.rem(me // 2 + 4 - d // 2, 4)
    core = lax.rem(lax.rem(me, 2) + lax.rem(d, 2), 2)
    return x * 2 + core


def each(low, high, body):
    def step(i, carry):
        body(i)
        return carry

    lax.fori_loop(low, high, step, 0)


def greet(nr, nc, row, col):
    barrier = pltpu.get_barrier_semaphore()
    each(1, nc, lambda d: pl.semaphore_signal(
        barrier, inc=1, device_id={"col": col_peer(col, d)}, device_id_type=pl.DeviceIdType.MESH))
    each(1, nr, lambda d: pl.semaphore_signal(
        barrier, inc=1, device_id={"row": row_peer(row, d)}, device_id_type=pl.DeviceIdType.MESH))
    pl.semaphore_wait(barrier, nc + nr - 2)


def share_kernel(nr, nc, asm, pinv, panel, pivot, chunk, ss1, rs1, ss2, rs2, ss3, rs3, ss4, rs4):
    row = lax.axis_index("row")
    col = lax.axis_index("col")
    mesh = pl.DeviceIdType.MESH
    pc = panel.shape[0] // nc
    vc = pivot.shape[0] // nr

    def rows_of(ref, index, size):
        return ref.at[pl.ds(pl.multiple_of(index * size, size), size)]

    def pivot_out(d):
        return pltpu.make_async_remote_copy(
            rows_of(asm, d, vc), rows_of(pivot, d, vc), ss1.at[d], rs1.at[0],
            device_id={"row": d}, device_id_type=mesh)

    def panel_out(d):
        return pltpu.make_async_remote_copy(
            rows_of(asm, d, pc), chunk, ss2.at[d], rs2.at[0],
            device_id={"col": d}, device_id_type=mesh)

    def pivot_share(d, whose):
        part = rows_of(pivot, whose, vc)
        return pltpu.make_async_remote_copy(
            part, part, ss3.at[d], rs3.at[d],
            device_id={"row": row_peer(row, d)}, device_id_type=mesh)

    def panel_share(d, whose):
        part = rows_of(panel, whose, pc)
        return pltpu.make_async_remote_copy(
            part, part, ss4.at[d], rs4.at[d],
            device_id={"col": col_peer(col, d)}, device_id_type=mesh)

    greet(nr, nc, row, col)

    @pl.when(col == 0)
    def _():
        each(1, nc, lambda d: panel_out(d).start())
        chunk[...] = asm[0:pc, :]

    @pl.when(row == 0)
    def _():
        each(1, nr, lambda d: pivot_out(d).start())
        pivot[0:vc, :] = asm[0:vc, :]

    @pl.when(row > 0)
    def _():
        pivot_out(row).wait_recv()

    each(1, nr, lambda d: pivot_share(d, row).start())

    @pl.when(col > 0)
    def _():
        panel_out(col).wait_recv()

    part = jnp.dot(chunk[...].astype(F32), pinv[...], precision=HI, preferred_element_type=F32)
    panel[pl.ds(pl.multiple_of(col * pc, pc), pc), :] = part.astype(BF)
    each(1, nc, lambda d: panel_share(d, col).start())

    each(1, nr, lambda d: pivot_share(d, row_from(row, d)).wait_recv())
    each(1, nc, lambda d: panel_share(d, col_from(col, d)).wait_recv())
    each(1, nr, lambda d: pivot_share(d, row).wait_send())
    each(1, nc, lambda d: panel_share(d, col).wait_send())

    @pl.when(col == 0)
    def _():
        each(1, nc, lambda d: panel_out(d).wait_send())

    @pl.when(row == 0)
    def _():
        each(1, nr, lambda d: pivot_out(d).wait_send())


def share(nr, nc, asm, pinv):
    rows, cols = asm.shape
    vmem = pl.BlockSpec(memory_space=pltpu.VMEM)
    dma = pltpu.SemaphoreType.DMA
    pw = pinv.shape[0]
    return pl.pallas_call(
        lambda *refs: share_kernel(nr, nc, *refs),
        out_shape=(
            jax.ShapeDtypeStruct((rows, pw), BF),
            jax.ShapeDtypeStruct((pw, cols), BF),
        ),
        in_specs=[vmem, vmem],
        out_specs=(vmem, vmem),
        scratch_shapes=[
            pltpu.VMEM((rows // nc, pw), BF),
            dma((nr,)), dma((1,)), dma((nc,)), dma((1,)),
            dma((nr,)), dma((nr,)), dma((nc,)), dma((nc,)),
        ],
        compiler_params=pltpu.CompilerParams(
            collective_id=0, has_side_effects=True, vmem_limit_bytes=32 * 1024 * 1024
        ),
        name="share",
    )(asm, pinv)


def nt(a, b):
    return lax.dot_general(a, b, (((1,), (1,)), ((), ())), preferred_element_type=F32)


def exchange_kernel(
    nr, nc, fr, fc, cs, rs,
    left, child, core, right, maps, xrecv,
    lbuf, mixing, tri, mask, slots, pick32, pick_cols, pick_rows, zsend, zrecv, xsend,
    ls, lr, zs, zr, xs, xr,
):
    row = lax.axis_index("row")
    col = lax.axis_index("col")
    mesh = pl.DeviceIdType.MESH
    i32 = jnp.int32
    nb, width = maps.shape[1:]
    half, quarter = width // 2, width // 4
    nt_steps = nb // 2
    y, z = col // 4, lax.rem(col, 4)

    def at(dy, dz):
        return lax.rem(y + dy + 4, 4) * 4 + lax.rem(z + dz + 4, 4)

    def off(h, p, s):
        return at(s, p) if h == 0 else at(p, s)

    def piece(h, block, part):
        size = half if part is None else quarter
        start = h * half + (0 if part is None else part * quarter)
        return pl.ds(pl.multiple_of(block * width + start, quarter), size)

    def hop(h, m, src_off, part, to):
        where = piece(h, off(h, *src_off), part)
        return pltpu.make_async_remote_copy(
            lbuf.at[where], lbuf.at[where], ls.at[h, m], lr.at[h, m],
            device_id={"col": off(h, *to)}, device_id_type=mesh)

    def arrived(h, m, src_off, part):
        where = piece(h, off(h, *src_off), part)
        pltpu.make_async_remote_copy(
            lbuf.at[where], lbuf.at[where], ls.at[h, m], lr.at[h, m],
            device_id={"col": col}, device_id_type=mesh).wait_recv()

    sent = []

    def go(h, m, src_off, part, to):
        copy = hop(h, m, src_off, part, to)
        copy.start()
        sent.append(copy)

    ks = (0, -1, 1, 2)

    def spread(h, n):
        go(h, 4 + 4 * n, (ks[n], 0), None, (0, 1))
        go(h, 5 + 4 * n, (ks[n], 0), None, (0, -1))

    def onward(h, n):
        arrived(h, 4 + 4 * n, (ks[n], -1), None)
        go(h, 6 + 4 * n, (ks[n], -1), 0, (0, 1))
        arrived(h, 5 + 4 * n, (ks[n], 1), None)
        go(h, 7 + 4 * n, (ks[n], 1), 1, (0, -1))

    def last(h, n):
        arrived(h, 6 + 4 * n, (ks[n], -2), 0)
        arrived(h, 7 + 4 * n, (ks[n], 2), 1)

    lbuf[pl.ds(pl.multiple_of(col * width, width), width), :] = left[...]
    greet(nr, nc, row, col)
    for h in range(2):
        go(h, 0, (0, 0), None, (1, 0))
        go(h, 1, (0, 0), None, (-1, 0))
    for h in range(2):
        spread(h, 0)

    mixing[...] = jnp.dot(core[...], right[...], preferred_element_type=F32).astype(BF)
    before = lax.broadcasted_iota(i32, (width, width), 0) < lax.broadcasted_iota(i32, (width, width), 1)
    tri[...] = jnp.where(before, 1.0, 0.0).astype(BF)

    for h in range(2):
        arrived(h, 0, (-1, 0), None)
        go(h, 2, (-1, 0), 0, (1, 0))
        arrived(h, 1, (1, 0), None)
        go(h, 3, (1, 0), 1, (-1, 0))
    for h in range(2):
        spread(h, 1)
        spread(h, 2)

    def ranks(rows):
        counted = jnp.dot(mask[0:rows, :].astype(BF), tri[...], preferred_element_type=F32)
        slots[0:rows, :] = jnp.where(mask[0:rows, :] > 0.5, counted, -1.0)

    own = maps[row, pl.ds(col, 1), :] // fc
    mask[0:nc, :] = jnp.where(own == lax.broadcasted_iota(i32, (nc, width), 0), 1.0, 0.0)
    ranks(nc)
    steps_c = lax.broadcasted_iota(i32, (cs, width), 0).astype(F32)
    for g in range(nc):
        pick32[g * cs : (g + 1) * cs, :] = jnp.where(slots[g : g + 1, :] == steps_c, 1.0, 0.0)
    pick_cols[...] = pick32[...].astype(BF)

    for h in range(2):
        onward(h, 0)

    groups = lax.broadcasted_iota(i32, (nr, width), 0)
    for b in range(nb):
        mask[b * nr : (b + 1) * nr, :] = jnp.where(maps[row, b : b + 1, :] // fr == groups, 1.0, 0.0)
    ranks(nb * nr)

    for h in range(2):
        arrived(h, 2, (-2, 0), 0)
        arrived(h, 3, (2, 0), 1)
        spread(h, 3)

    steps_r = lax.broadcasted_iota(i32, (rs, width), 0).astype(F32)

    def make_rows(b):
        eight = slots[pl.ds(pl.multiple_of(b * nr, nr), nr), :]
        for g in range(nr):
            hit = jnp.where(eight[g : g + 1, :] == steps_r, 1.0, 0.0)
            pick_rows[b, g * rs : (g + 1) * rs, :] = hit.astype(BF)

    each(0, nb, make_rows)

    for h in range(2):
        onward(h, 1)
        onward(h, 2)
    for h in range(2):
        onward(h, 3)
    for n in range(4):
        for h in range(2):
            last(h, n)

    def col_copy(t, d, to, whose):
        return pltpu.make_async_remote_copy(
            zsend.at[t, to], zrecv.at[t, whose], zs.at[t, d], zr.at[t, d],
            device_id={"col": to}, device_id_type=mesh)

    def produce(t):
        rows = pl.ds(pl.multiple_of(t * 2 * width, 2 * width), 2 * width)
        product = jnp.dot(lbuf[rows, :], mixing[...], preferred_element_type=F32)
        update = (child[rows, :].astype(F32) - product).astype(BF)
        picked = nt(pick_cols[...], update).reshape(nc, cs // 8, 8, 2 * width)
        low = picked[:, :, None, :, :width]
        high = picked[:, :, None, :, width:]
        both = jnp.concatenate([low, high], axis=2).reshape(nc, 2 * cs, width)
        zsend[t] = both.astype(BF)
        zrecv[t, col] = zsend[t, col]
        each(1, nc, lambda d: col_copy(t, d, col_peer(col, d), col).start())

    each(0, nt_steps, produce)

    def row_copy(t, d, to, whose):
        return pltpu.make_async_remote_copy(
            xsend.at[t, to], xrecv.at[whose, t], xs.at[t, d], xr.at[t, d],
            device_id={"row": to}, device_id_type=mesh)

    def forward(t):
        each(1, nc, lambda d: col_copy(t, d, col_from(col, d), col_from(col, d)).wait_recv())
        got = zrecv[t].astype(F32).reshape(nc, cs // 8, 2, 8, width)
        for h in range(2):
            part = got[:, :, h].reshape(nc * cs, width).astype(BF)
            rows = nt(pick_rows[2 * t + h], part)
            xsend[t, :, h * rs : (h + 1) * rs, :] = rows.reshape(nr, rs, nc * cs).astype(BF)
        xrecv[row, t] = xsend[t, row]
        each(1, nr, lambda d: row_copy(t, d, row_peer(row, d), row).start())

    each(0, nt_steps, forward)

    def finish(t):
        each(1, nr, lambda d: row_copy(t, d, row_from(row, d), row_from(row, d)).wait_recv())
        each(1, nr, lambda d: row_copy(t, d, row_peer(row, d), row).wait_send())
        each(1, nc, lambda d: col_copy(t, d, col_peer(col, d), col).wait_send())

    each(0, nt_steps, finish)
    for copy in sent:
        copy.wait_send()


def exchange(nr, nc, fr, fc, cs, rs, left, child, core, right, maps):
    order, width = child.shape
    rank = left.shape[1]
    nb = order // width
    vmem = pl.BlockSpec(memory_space=pltpu.VMEM)
    dma = pltpu.SemaphoreType.DMA
    return pl.pallas_call(
        lambda *refs: exchange_kernel(nr, nc, fr, fc, cs, rs, *refs),
        out_shape=jax.ShapeDtypeStruct((nr, nb // 2, 2 * rs, nc * cs), BF),
        in_specs=[vmem] * 5,
        out_specs=vmem,
        scratch_shapes=[
            pltpu.VMEM((order, rank), BF),
            pltpu.VMEM((rank, width), BF),
            pltpu.VMEM((width, width), BF),
            pltpu.VMEM((nb * nr, width), F32),
            pltpu.VMEM((nb * nr, width), F32),
            pltpu.VMEM((nc * cs, width), F32),
            pltpu.VMEM((nc * cs, width), BF),
            pltpu.VMEM((nb, nr * rs, width), BF),
            pltpu.VMEM((nb // 2, nc, 2 * cs, width), BF),
            pltpu.VMEM((nb // 2, nc, 2 * cs, width), BF),
            pltpu.VMEM((nb // 2, nr, 2 * rs, nc * cs), BF),
            dma((2, 20)), dma((2, 20)),
            dma((nb // 2, nc)), dma((nb // 2, nc)),
            dma((nb // 2, nr)), dma((nb // 2, nr)),
        ],
        compiler_params=pltpu.CompilerParams(
            collective_id=1, has_side_effects=True, vmem_limit_bytes=56 * 1024 * 1024
        ),
        name="exchange",
    )(left, child, core, right, maps)


def on_device(
    child_block, left_gen, core_gen, right_gen, child_maps, parent_entries, pivot_inverse
):
    nr = lax.axis_size("row")
    nc = lax.axis_size("col")
    row_me = lax.axis_index("row")
    col_me = lax.axis_index("col")
    order = child_block.shape[1]
    width = child_block.shape[2]
    fr, fc = parent_entries.shape
    unit = order // (16 * nr * nr)
    cs = 6 * unit
    rs = 12 * unit
    pw = pivot_inverse.shape[0]
    nb = order // width

    blocks = child_maps.reshape(nr, nb, width)
    pos = jnp.arange(width, dtype=jnp.int32)
    tri = (pos[:, None] < pos[None, :]).astype(BF)
    rmask2 = (blocks // fr) == row_me
    rtarget = slot_targets(block_slots(rmask2, tri), blocks - row_me * fr, rs).reshape(nr * nb * rs)
    place_rows = (rtarget[None, :] == jnp.arange(fr, dtype=jnp.int32)[:, None]).astype(BF)
    cmask2 = (blocks // fc) == col_me
    ctarget = slot_targets(block_slots(cmask2, tri), blocks - col_me * fc, cs).reshape(nr, nb * cs)
    place_cols = (ctarget[:, :, None] == jnp.arange(fc, dtype=jnp.int32)[None, None, :]).astype(BF)

    moved = exchange(
        nr, nc, fr, fc, cs, rs, left_gen[0], child_block[0], core_gen[0], right_gen[0], blocks
    ).reshape(nr, nb * rs, nc * cs)
    wide = jnp.einsum("nsc,ncf->nsf", moved, place_cols, preferred_element_type=F32).astype(BF)
    placed = jnp.dot(place_rows, wide.reshape(nr * nb * rs, fc), preferred_element_type=F32)
    assembled = parent_entries.astype(F32) + placed

    panel_rows, pivot = share(nr, nc, assembled.astype(BF), pivot_inverse)
    local_panel = lax.cond(
        col_me == 0,
        lambda: jnp.dot(assembled, pivot_inverse, precision=HI, preferred_element_type=F32),
        lambda: jnp.zeros((fr, pw), F32),
    )
    trailing = assembled - jnp.dot(panel_rows, pivot, preferred_element_type=F32)
    global_rows = row_me * fr + jnp.arange(fr, dtype=jnp.int32)
    lower = jnp.where(col_me == 0, local_panel, trailing)
    return jnp.where(global_rows[:, None] < pw, assembled, lower)


def solution(mesh):
    return jax.shard_map(
        on_device,
        mesh=mesh,
        in_specs=(
            P("row", None, "col"),
            P("row", "col", None),
            P("row", None, None),
            P("row", None, "col"),
            P(),
            P("row", "col"),
            P(),
        ),
        out_specs=P("row", "col"),
        check_vma=False,
    )
```

```python
import jax
import jax.numpy as jnp
from jax import lax
from jax.experimental import pallas as pl
from jax.experimental.pallas import tpu as pltpu
from jax.sharding import PartitionSpec as P

BF = jnp.bfloat16
F32 = jnp.float32
HI = lax.Precision.HIGHEST


def block_slots(mask, tri):
    ranks = jnp.dot(mask.astype(BF), tri, preferred_element_type=F32).astype(jnp.int32)
    return jnp.where(mask, ranks, -1)


def slot_targets(slots, targets, count):
    hit = slots[..., None, :] == jnp.arange(count, dtype=jnp.int32)[:, None]
    return jnp.sum(jnp.where(hit, targets[..., None, :] + 1, 0), axis=-1) - 1


def col_peer(me, d):
    y = lax.rem(me // 4 + d // 4, 4)
    z = lax.rem(lax.rem(me, 4) + lax.rem(d, 4), 4)
    return y * 4 + z


def row_peer(me, d):
    x = lax.rem(me // 2 + d // 2, 4)
    core = lax.rem(lax.rem(me, 2) + lax.rem(d, 2), 2)
    return x * 2 + core


def col_from(me, d):
    y = lax.rem(me // 4 + 4 - d // 4, 4)
    z = lax.rem(lax.rem(me, 4) + 4 - lax.rem(d, 4), 4)
    return y * 4 + z


def row_from(me, d):
    x = lax.rem(me // 2 + 4 - d // 2, 4)
    core = lax.rem(lax.rem(me, 2) + lax.rem(d, 2), 2)
    return x * 2 + core


def each(low, high, body):
    def step(i, carry):
        body(i)
        return carry

    lax.fori_loop(low, high, step, 0)


def greet(nr, nc, row, col):
    barrier = pltpu.get_barrier_semaphore()
    each(1, nc, lambda d: pl.semaphore_signal(
        barrier, inc=1, device_id={"col": col_peer(col, d)}, device_id_type=pl.DeviceIdType.MESH))
    each(1, nr, lambda d: pl.semaphore_signal(
        barrier, inc=1, device_id={"row": row_peer(row, d)}, device_id_type=pl.DeviceIdType.MESH))
    pl.semaphore_wait(barrier, nc + nr - 2)


def share_kernel(nr, nc, full, pinv, panel, pivot, own_panel, asm, top, chunk, ss1, rs1, ss2, rs2, ss3, rs3, ss4, rs4):
    row = lax.axis_index("row")
    col = lax.axis_index("col")
    mesh = pl.DeviceIdType.MESH
    pc = panel.shape[0] // nc
    vc = pivot.shape[0] // nr

    def rows_of(ref, index, size):
        return ref.at[pl.ds(pl.multiple_of(index * size, size), size)]

    def pivot_out(d):
        return pltpu.make_async_remote_copy(
            rows_of(top, d, vc), rows_of(pivot, d, vc), ss1.at[d], rs1.at[0],
            device_id={"row": d}, device_id_type=mesh)

    def panel_out(d):
        return pltpu.make_async_remote_copy(
            rows_of(asm, d, pc), chunk, ss2.at[d], rs2.at[0],
            device_id={"col": d}, device_id_type=mesh)

    def pivot_share(d, whose):
        part = rows_of(pivot, whose, vc)
        return pltpu.make_async_remote_copy(
            part, part, ss3.at[d], rs3.at[d],
            device_id={"row": row_peer(row, d)}, device_id_type=mesh)

    def panel_share(d, whose):
        part = rows_of(panel, whose, pc)
        return pltpu.make_async_remote_copy(
            part, part, ss4.at[d], rs4.at[d],
            device_id={"col": col_peer(col, d)}, device_id_type=mesh)

    greet(nr, nc, row, col)

    @pl.when(col == 0)
    def _():
        asm[...] = full[...].astype(BF)
        each(1, nc, lambda d: panel_out(d).start())
        chunk[...] = asm[0:pc, :]

    @pl.when(row == 0)
    def _():
        top[...] = full[0 : vc * nr, :].astype(BF)
        each(1, nr, lambda d: pivot_out(d).start())
        pivot[0:vc, :] = top[0:vc, :]

    @pl.when(row > 0)
    def _():
        pivot_out(row).wait_recv()

    each(1, nr, lambda d: pivot_share(d, row).start())

    @pl.when(col > 0)
    def _():
        panel_out(col).wait_recv()

    part = jnp.dot(chunk[...].astype(F32), pinv[...], precision=HI, preferred_element_type=F32)
    panel[pl.ds(pl.multiple_of(col * pc, pc), pc), :] = part.astype(BF)
    each(1, nc, lambda d: panel_share(d, col).start())

    @pl.when(col == 0)
    def _():
        def rows_panel(i):
            rows = pl.ds(pl.multiple_of(i * 256, 256), 256)
            own_panel[rows, :] = jnp.dot(
                full[rows, :], pinv[...], precision=HI, preferred_element_type=F32)

        each(0, full.shape[0] // 256, rows_panel)

    each(1, nr, lambda d: pivot_share(d, row_from(row, d)).wait_recv())
    each(1, nc, lambda d: panel_share(d, col_from(col, d)).wait_recv())
    each(1, nr, lambda d: pivot_share(d, row).wait_send())
    each(1, nc, lambda d: panel_share(d, col).wait_send())

    @pl.when(col == 0)
    def _():
        each(1, nc, lambda d: panel_out(d).wait_send())

    @pl.when(row == 0)
    def _():
        each(1, nr, lambda d: pivot_out(d).wait_send())


def share(nr, nc, asm, pinv):
    rows, cols = asm.shape
    vmem = pl.BlockSpec(memory_space=pltpu.VMEM)
    dma = pltpu.SemaphoreType.DMA
    pw = pinv.shape[0]
    return pl.pallas_call(
        lambda *refs: share_kernel(nr, nc, *refs),
        out_shape=(
            jax.ShapeDtypeStruct((rows, pw), BF),
            jax.ShapeDtypeStruct((pw, cols), BF),
            jax.ShapeDtypeStruct((rows, pw), F32),
        ),
        in_specs=[vmem, vmem],
        out_specs=(vmem, vmem, vmem),
        scratch_shapes=[
            pltpu.VMEM((rows, cols), BF),
            pltpu.VMEM((pw, cols), BF),
            pltpu.VMEM((rows // nc, pw), BF),
            dma((nr,)), dma((1,)), dma((nc,)), dma((1,)),
            dma((nr,)), dma((nr,)), dma((nc,)), dma((nc,)),
        ],
        compiler_params=pltpu.CompilerParams(
            collective_id=0, has_side_effects=True, vmem_limit_bytes=32 * 1024 * 1024
        ),
        name="share",
    )(asm, pinv)


def nt(a, b):
    return lax.dot_general(a, b, (((1,), (1,)), ((), ())), preferred_element_type=F32)


def exchange_kernel(
    nr, nc, fr, fc, cs, rs,
    left, child, core, right, maps, xrecv,
    lbuf, msel, product, tri, mask, slots, pick32, pick_cols, pick_rows, zsend, zrecv, xsend,
    ls, lr, zs, zr, xs, xr,
):
    row = lax.axis_index("row")
    col = lax.axis_index("col")
    mesh = pl.DeviceIdType.MESH
    i32 = jnp.int32
    nb, width = maps.shape[1:]
    half, quarter = width // 2, width // 4
    steps = nb // 2
    y, z = col // 4, lax.rem(col, 4)

    def at(dy, dz):
        return lax.rem(y + dy + 4, 4) * 4 + lax.rem(z + dz + 4, 4)

    def off(h, p, s):
        return at(s, p) if h == 0 else at(p, s)

    def piece(h, block, part):
        size = half if part is None else quarter
        start = h * half + (0 if part is None else part * quarter)
        return pl.ds(pl.multiple_of(block * width + start, quarter), size)

    def hop(h, m, src_off, part, to):
        where = piece(h, off(h, *src_off), part)
        return pltpu.make_async_remote_copy(
            lbuf.at[where], lbuf.at[where], ls.at[h, m], lr.at[h, m],
            device_id={"col": off(h, *to)}, device_id_type=mesh)

    def arrived(h, m, src_off, part):
        where = piece(h, off(h, *src_off), part)
        pltpu.make_async_remote_copy(
            lbuf.at[where], lbuf.at[where], ls.at[h, m], lr.at[h, m],
            device_id={"col": col}, device_id_type=mesh).wait_recv()

    sent = []

    def go(h, m, src_off, part, to):
        copy = hop(h, m, src_off, part, to)
        copy.start()
        sent.append(copy)

    ks = (0, -1, 1, 2)

    def spread(h, n):
        go(h, 4 + 4 * n, (ks[n], 0), None, (0, 1))
        go(h, 5 + 4 * n, (ks[n], 0), None, (0, -1))

    def onward(h, n):
        arrived(h, 4 + 4 * n, (ks[n], -1), None)
        go(h, 6 + 4 * n, (ks[n], -1), 0, (0, 1))
        arrived(h, 5 + 4 * n, (ks[n], 1), None)
        go(h, 7 + 4 * n, (ks[n], 1), 1, (0, -1))

    def last(h, n):
        arrived(h, 6 + 4 * n, (ks[n], -2), 0)
        arrived(h, 7 + 4 * n, (ks[n], 2), 1)

    def pair_of(who, k):
        kk = k // 2
        dy = kk + kk // 2 - 2 * (kk // 3)
        return lax.rem(who // 4 + dy, 4) * 2 + lax.rem(lax.rem(who, 4) // 2 + lax.rem(k, 2), 2)

    def col_copy(k, d, to, whose):
        t = pair_of(to, k)
        return pltpu.make_async_remote_copy(
            zsend.at[t, to], zrecv.at[t, whose], zs.at[k, d], zr.at[k, d],
            device_id={"col": to}, device_id_type=mesh)

    def mix_copy(d, to, whose):
        return pltpu.make_async_remote_copy(
            zsend.at[steps, to], zrecv.at[steps, whose], zs.at[steps, d], zr.at[steps, d],
            device_id={"col": to}, device_id_type=mesh)

    def issue(k):
        each(1, nc, lambda d: col_copy(k, d, col_peer(col, d), col).start())

    def pick(t, rows):
        picked = nt(pick_cols[...], rows).reshape(nc, cs // 8, 8, 2 * width)
        low = picked[:, :, None, :, :width]
        high = picked[:, :, None, :, width:]
        both = jnp.concatenate([low, high], axis=2).reshape(nc, 2 * cs, width)
        zsend[t] = both.astype(BF)
        zrecv[t, col] = zsend[t, col]

    def parts(t):
        got = zrecv[t].astype(F32).reshape(nc, cs // 8, 2, 8, width)
        return [got[:, :, h].reshape(nc * cs, width) for h in range(2)]

    def ranks(rows):
        counted = jnp.dot(mask[0:rows, :].astype(BF), tri[...], preferred_element_type=F32)
        slots[0:rows, :] = jnp.where(mask[0:rows, :] > 0.5, counted, -1.0)

    steps_r = lax.broadcasted_iota(i32, (rs, width), 0).astype(F32)

    def row_copy(k, d, to, whose):
        t = pair_of(col, k)
        return pltpu.make_async_remote_copy(
            xsend.at[t, to], xrecv.at[whose, t], xs.at[k, d], xr.at[k, d],
            device_id={"row": to}, device_id_type=mesh)

    def forward(k):
        t = pair_of(col, k)
        for h in range(2):
            eight = slots[pl.ds(pl.multiple_of((2 * t + h) * nr, nr), nr), :]
            for g in range(nr):
                hit = jnp.where(eight[g : g + 1, :] == steps_r, 1.0, 0.0)
                pick_rows[h, g * rs : (g + 1) * rs, :] = hit.astype(BF)
        rows = pl.ds(pl.multiple_of(t * 2 * width, 2 * width), 2 * width)
        product[...] = nt(msel[...], lbuf[rows, :])
        each(1, nc, lambda d: col_copy(k, d, col, col_from(col, d)).wait_recv())
        got = parts(t)
        for h in range(2):
            update = (got[h] - product[:, h * width : (h + 1) * width]).astype(BF)
            chosen = nt(pick_rows[h], update)
            xsend[t, :, h * rs : (h + 1) * rs, :] = chosen.reshape(nr, rs, nc * cs).astype(BF)
        xrecv[row, t] = xsend[t, row]
        each(1, nr, lambda d: row_copy(k, d, row_peer(row, d), row).start())

    lbuf[pl.ds(pl.multiple_of(col * width, width), width), :] = left[...]
    greet(nr, nc, row, col)
    for h in range(2):
        go(h, 0, (0, 0), None, (1, 0))
        go(h, 1, (0, 0), None, (-1, 0))
    for h in range(2):
        spread(h, 0)

    before = lax.broadcasted_iota(i32, (width, width), 0) < lax.broadcasted_iota(i32, (width, width), 1)
    tri[...] = jnp.where(before, 1.0, 0.0).astype(BF)
    own = maps[row, pl.ds(col, 1), :] // fc
    mask[0:nc, :] = jnp.where(own == lax.broadcasted_iota(i32, (nc, width), 0), 1.0, 0.0)
    ranks(nc)
    steps_c = lax.broadcasted_iota(i32, (cs, width), 0).astype(F32)
    for g in range(nc):
        pick32[g * cs : (g + 1) * cs, :] = jnp.where(slots[g : g + 1, :] == steps_c, 1.0, 0.0)
    pick_cols[...] = pick32[...].astype(BF)
    mixing = jnp.dot(core[...], right[...], preferred_element_type=F32).astype(BF)
    pick(steps, mixing)
    each(1, nc, lambda d: mix_copy(d, col_peer(col, d), col).start())
    each(0, steps, lambda t: pick(
        t, child[pl.ds(pl.multiple_of(t * 2 * width, 2 * width), 2 * width), :]))
    issue(0)
    for h in range(2):
        arrived(h, 0, (-1, 0), None)
        go(h, 2, (-1, 0), 0, (1, 0))
        arrived(h, 1, (1, 0), None)
        go(h, 3, (1, 0), 1, (-1, 0))
    for h in range(2):
        spread(h, 1)
        spread(h, 2)
    for h in range(2):
        onward(h, 0)
    issue(1)

    groups = lax.broadcasted_iota(i32, (nr, width), 0)
    for b in range(nb):
        mask[b * nr : (b + 1) * nr, :] = jnp.where(maps[row, b : b + 1, :] // fr == groups, 1.0, 0.0)
    ranks(nb * nr)
    each(1, nc, lambda d: mix_copy(d, col, col_from(col, d)).wait_recv())
    low, high = parts(steps)
    msel[:, :width] = low.astype(BF)
    msel[:, width:] = high.astype(BF)

    forward(0)
    for h in range(2):
        arrived(h, 2, (-2, 0), 0)
        arrived(h, 3, (2, 0), 1)
        spread(h, 3)
    for h in range(2):
        last(h, 0)
        onward(h, 1)
        onward(h, 2)
    issue(2)
    issue(3)
    forward(1)
    for h in range(2):
        onward(h, 3)
    for h in range(2):
        last(h, 1)
        last(h, 2)
    issue(4)
    issue(5)
    forward(2)
    for h in range(2):
        last(h, 3)
    issue(6)
    issue(7)
    each(3, steps, forward)

    def finish(k):
        each(1, nr, lambda d: row_copy(k, d, row, row_from(row, d)).wait_recv())
        each(1, nr, lambda d: row_copy(k, d, row_peer(row, d), row).wait_send())
        each(1, nc, lambda d: col_copy(k, d, col_peer(col, d), col).wait_send())

    each(0, steps, finish)
    each(1, nc, lambda d: mix_copy(d, col_peer(col, d), col).wait_send())
    for copy in sent:
        copy.wait_send()


def exchange(nr, nc, fr, fc, cs, rs, left, child, core, right, maps):
    order, width = child.shape
    rank = left.shape[1]
    nb = order // width
    vmem = pl.BlockSpec(memory_space=pltpu.VMEM)
    dma = pltpu.SemaphoreType.DMA
    return pl.pallas_call(
        lambda *refs: exchange_kernel(nr, nc, fr, fc, cs, rs, *refs),
        out_shape=jax.ShapeDtypeStruct((nr, nb // 2, 2 * rs, nc * cs), BF),
        in_specs=[vmem] * 5,
        out_specs=vmem,
        scratch_shapes=[
            pltpu.VMEM((order, rank), BF),
            pltpu.VMEM((nc * cs, rank), BF),
            pltpu.VMEM((nc * cs, 2 * width), F32),
            pltpu.VMEM((width, width), BF),
            pltpu.VMEM((nb * nr, width), F32),
            pltpu.VMEM((nb * nr, width), F32),
            pltpu.VMEM((nc * cs, width), F32),
            pltpu.VMEM((nc * cs, width), BF),
            pltpu.VMEM((2, nr * rs, width), BF),
            pltpu.VMEM((nb // 2 + 1, nc, 2 * cs, width), BF),
            pltpu.VMEM((nb // 2 + 1, nc, 2 * cs, width), BF),
            pltpu.VMEM((nb // 2, nr, 2 * rs, nc * cs), BF),
            dma((2, 20)), dma((2, 20)),
            dma((nb // 2 + 1, nc)), dma((nb // 2 + 1, nc)),
            dma((nb // 2, nr)), dma((nb // 2, nr)),
        ],
        compiler_params=pltpu.CompilerParams(
            collective_id=1, has_side_effects=True, vmem_limit_bytes=56 * 1024 * 1024
        ),
        name="exchange",
    )(left, child, core, right, maps)


def on_device(
    child_block, left_gen, core_gen, right_gen, child_maps, parent_entries, pivot_inverse
):
    nr = lax.axis_size("row")
    nc = lax.axis_size("col")
    row_me = lax.axis_index("row")
    col_me = lax.axis_index("col")
    order = child_block.shape[1]
    width = child_block.shape[2]
    fr, fc = parent_entries.shape
    unit = order // (16 * nr * nr)
    cs = 6 * unit
    rs = 12 * unit
    pw = pivot_inverse.shape[0]
    nb = order // width

    blocks = child_maps.reshape(nr, nb, width)
    pos = jnp.arange(width, dtype=jnp.int32)
    tri = (pos[:, None] < pos[None, :]).astype(BF)
    rmask2 = (blocks // fr) == row_me
    rtarget = slot_targets(block_slots(rmask2, tri), blocks - row_me * fr, rs).reshape(nr * nb * rs)
    place_rows = (rtarget[None, :] == jnp.arange(fr, dtype=jnp.int32)[:, None]).astype(BF)
    cmask2 = (blocks // fc) == col_me
    ctarget = slot_targets(block_slots(cmask2, tri), blocks - col_me * fc, cs).reshape(nr, nb * cs)
    place_cols = (ctarget[:, :, None] == jnp.arange(fc, dtype=jnp.int32)[None, None, :]).astype(BF)

    moved = exchange(
        nr, nc, fr, fc, cs, rs, left_gen[0], child_block[0], core_gen[0], right_gen[0], blocks
    ).reshape(nr, nb * rs, nc * cs)
    wide = jnp.einsum("nsc,ncf->nsf", moved, place_cols, preferred_element_type=F32).astype(BF)
    placed = jnp.dot(place_rows, wide.reshape(nr * nb * rs, fc), preferred_element_type=F32)
    assembled = parent_entries.astype(F32) + placed

    panel_rows, pivot, local_panel = share(nr, nc, assembled, pivot_inverse)
    trailing = assembled - jnp.dot(panel_rows, pivot, preferred_element_type=F32)
    global_rows = row_me * fr + jnp.arange(fr, dtype=jnp.int32)
    lower = jnp.where(col_me == 0, local_panel, trailing)
    return jnp.where(global_rows[:, None] < pw, assembled, lower)


def solution(mesh):
    return jax.shard_map(
        on_device,
        mesh=mesh,
        in_specs=(
            P("row", None, "col"),
            P("row", "col", None),
            P("row", None, None),
            P("row", None, "col"),
            P(),
            P("row", "col"),
            P(),
        ),
        out_specs=P("row", "col"),
        check_vma=False,
    )
```

```python
import jax
import jax.numpy as jnp
from jax import lax
from jax.experimental import pallas as pl
from jax.experimental.pallas import tpu as pltpu
from jax.sharding import PartitionSpec as P

BF = jnp.bfloat16
F32 = jnp.float32
HI = lax.Precision.HIGHEST


def col_peer(me, d):
    y = lax.rem(me // 4 + d // 4, 4)
    z = lax.rem(lax.rem(me, 4) + lax.rem(d, 4), 4)
    return y * 4 + z


def row_peer(me, d):
    x = lax.rem(me // 2 + d // 2, 4)
    core = lax.rem(lax.rem(me, 2) + lax.rem(d, 2), 2)
    return x * 2 + core


def col_from(me, d):
    y = lax.rem(me // 4 + 4 - d // 4, 4)
    z = lax.rem(lax.rem(me, 4) + 4 - lax.rem(d, 4), 4)
    return y * 4 + z


def row_from(me, d):
    x = lax.rem(me // 2 + 4 - d // 2, 4)
    core = lax.rem(lax.rem(me, 2) + lax.rem(d, 2), 2)
    return x * 2 + core


def each(low, high, body):
    def step(i, carry):
        body(i)
        return carry

    lax.fori_loop(low, high, step, 0)


def greet(nr, nc, row, col):
    barrier = pltpu.get_barrier_semaphore()
    each(1, nc, lambda d: pl.semaphore_signal(
        barrier, inc=1, device_id={"col": col_peer(col, d)}, device_id_type=pl.DeviceIdType.MESH))
    each(1, nr, lambda d: pl.semaphore_signal(
        barrier, inc=1, device_id={"row": row_peer(row, d)}, device_id_type=pl.DeviceIdType.MESH))
    pl.semaphore_wait(barrier, nc + nr - 2)


def nt(a, b):
    return lax.dot_general(a, b, (((1,), (1,)), ((), ())), preferred_element_type=F32)


def front_kernel(
    nr, nc, fr, fc, cs, rs,
    left, child_in, core, right, maps, parent_in, pinv_in,
    asm, panel, pivot, own_panel,
    child, parent, pinv, lbuf, msel, product, tri, mask, slots, far_slots, digits, sel,
    pick32, pick_cols, pick_rows, row_at, col_at, place_cols, place_rows, wide,
    zsend, zrecv, xsend, xrecv, asm16, top16, chunk,
    ls, lr, zs, zr, xs, xr, ss1, rs1, ss2, rs2, ss3, rs3, ss4, rs4, loads,
):
    row = lax.axis_index("row")
    col = lax.axis_index("col")
    mesh = pl.DeviceIdType.MESH
    i32 = jnp.int32
    width = child.shape[1]
    nb = child.shape[0] // width
    half, quarter = width // 2, width // 4
    steps = nb // 2
    y, z = col // 4, lax.rem(col, 4)

    def at(dy, dz):
        return lax.rem(y + dy + 4, 4) * 4 + lax.rem(z + dz + 4, 4)

    def off(h, p, s):
        return at(s, p) if h == 0 else at(p, s)

    def piece(h, block, part):
        size = half if part is None else quarter
        start = h * half + (0 if part is None else part * quarter)
        return pl.ds(pl.multiple_of(block * width + start, quarter), size)

    def hop(h, m, src_off, part, to):
        where = piece(h, off(h, *src_off), part)
        return pltpu.make_async_remote_copy(
            lbuf.at[where], lbuf.at[where], ls.at[h, m], lr.at[h, m],
            device_id={"col": off(h, *to)}, device_id_type=mesh)

    def arrived(h, m, src_off, part):
        where = piece(h, off(h, *src_off), part)
        pltpu.make_async_remote_copy(
            lbuf.at[where], lbuf.at[where], ls.at[h, m], lr.at[h, m],
            device_id={"col": col}, device_id_type=mesh).wait_recv()

    sent = []

    def go(h, m, src_off, part, to):
        copy = hop(h, m, src_off, part, to)
        copy.start()
        sent.append(copy)

    ks = (0, -1, 1, 2)

    def spread(h, n):
        go(h, 4 + 4 * n, (ks[n], 0), None, (0, 1))
        go(h, 5 + 4 * n, (ks[n], 0), None, (0, -1))

    def onward(h, n):
        arrived(h, 4 + 4 * n, (ks[n], -1), None)
        go(h, 6 + 4 * n, (ks[n], -1), 0, (0, 1))
        arrived(h, 5 + 4 * n, (ks[n], 1), None)
        go(h, 7 + 4 * n, (ks[n], 1), 1, (0, -1))

    def last(h, n):
        arrived(h, 6 + 4 * n, (ks[n], -2), 0)
        arrived(h, 7 + 4 * n, (ks[n], 2), 1)

    def pair_of(who, k):
        kk = k // 2
        dy = kk + kk // 2 - 2 * (kk // 3)
        return lax.rem(who // 4 + dy, 4) * 2 + lax.rem(lax.rem(who, 4) // 2 + lax.rem(k, 2), 2)

    def col_copy(k, d, to, whose):
        t = pair_of(to, k)
        return pltpu.make_async_remote_copy(
            zsend.at[t, to], zrecv.at[t, whose], zs.at[k, d], zr.at[k, d],
            device_id={"col": to}, device_id_type=mesh)

    def mix_copy(d, to, whose):
        return pltpu.make_async_remote_copy(
            zsend.at[steps, to], zrecv.at[steps, whose], zs.at[steps, d], zr.at[steps, d],
            device_id={"col": to}, device_id_type=mesh)

    def issue(k):
        each(1, nc, lambda d: col_copy(k, d, col_peer(col, d), col).start())

    def pick(t, rows):
        picked = nt(pick_cols[...], rows).reshape(nc, cs // 8, 8, 2 * width)
        low = picked[:, :, None, :, :width]
        high = picked[:, :, None, :, width:]
        both = jnp.concatenate([low, high], axis=2).reshape(nc, 2 * cs, width)
        zsend[t] = both.astype(BF)
        zrecv[t, col] = zsend[t, col]

    def parts(t):
        got = zrecv[t].astype(F32).reshape(nc, cs // 8, 2, 8, width)
        return [got[:, :, h].reshape(nc * cs, width) for h in range(2)]

    def ranks(rows, into):
        counted = jnp.dot(mask[0:rows, :].astype(BF), tri[...], preferred_element_type=F32)
        into[0:rows, :] = jnp.where(mask[0:rows, :] > 0.5, counted, -1.0)

    steps_r = lax.broadcasted_iota(i32, (rs, width), 0).astype(F32)

    def row_copy(k, d, to, whose):
        t = pair_of(col, k)
        return pltpu.make_async_remote_copy(
            xsend.at[t, to], xrecv.at[whose, t], xs.at[k, d], xr.at[k, d],
            device_id={"row": to}, device_id_type=mesh)

    def forward(k):
        t = pair_of(col, k)
        for h in range(2):
            eight = slots[pl.ds(pl.multiple_of((2 * t + h) * nr, nr), nr), :]
            for g in range(nr):
                hit = jnp.where(eight[g : g + 1, :] == steps_r, 1.0, 0.0)
                pick_rows[h, g * rs : (g + 1) * rs, :] = hit.astype(BF)
        rows = pl.ds(pl.multiple_of(t * 2 * width, 2 * width), 2 * width)
        product[...] = nt(msel[...], lbuf[rows, :])
        each(1, nc, lambda d: col_copy(k, d, col, col_from(col, d)).wait_recv())
        got = parts(t)
        for h in range(2):
            update = (got[h] - product[:, h * width : (h + 1) * width]).astype(BF)
            chosen = nt(pick_rows[h], update)
            xsend[t, :, h * rs : (h + 1) * rs, :] = chosen.reshape(nr, rs, nc * cs).astype(BF)
        xrecv[row, t] = xsend[t, row]
        each(1, nr, lambda d: row_copy(k, d, row_peer(row, d), row).start())

    def split(targets):
        high = targets // 32
        return high.astype(F32), (targets - high * 32).astype(F32)

    def far_rows():
        for b in range(nb):
            here = maps[:, b * width : (b + 1) * width]
            mask[b * nr : (b + 1) * nr, :] = jnp.where(here // fr == row, 1.0, 0.0)
            high, low = split(here - row * fr + 1)
            digits[b] = jnp.concatenate([high, low], axis=0).astype(BF)
        ranks(nb * nr, far_slots)
        size = nr * rs
        sub = lax.broadcasted_iota(i32, (2 * nr, size), 0)
        lane = lax.broadcasted_iota(i32, (2 * nr, size), 1)
        weight = jnp.where(lane // rs == lax.rem(sub, nr), jnp.where(sub < nr, 32.0, 1.0), 0.0)

        def one(b):
            eight = far_slots[pl.ds(pl.multiple_of(b * nr, nr), nr), :]
            for g in range(nr):
                hit = jnp.where(eight[g : g + 1, :] == steps_r, 1.0, 0.0)
                sel[g * rs : (g + 1) * rs, :] = hit.astype(BF)
            found = nt(digits[b], sel[...]) * weight
            row_at[pl.ds(b, 1), :] = jnp.sum(found, axis=0, keepdims=True) - 1.0

        each(0, nb, one)

    def far_cols():
        size = nc * cs
        sub = lax.broadcasted_iota(i32, (2 * nc, size), 0)
        lane = lax.broadcasted_iota(i32, (2 * nc, size), 1)
        weight = jnp.where(lane // cs == lax.rem(sub, nc), jnp.where(sub < nc, 32.0, 1.0), 0.0)
        spots = lax.broadcasted_iota(i32, (fc, size), 0).astype(F32)

        def one(c):
            for q in range(nc):
                here = maps[pl.ds(c, 1), q * width : (q + 1) * width]
                mask[q : q + 1, :] = jnp.where(here // fc == col, 1.0, 0.0)
                high, low = split(here - col * fc + 1)
                pick32[q : q + 1, :] = high
                pick32[nc + q : nc + q + 1, :] = low
            both = pick32[0 : 2 * nc, :].astype(BF)
            ranks(nc, far_slots)
            for q in range(nc):
                hit = jnp.where(far_slots[q : q + 1, :] == steps_c, 1.0, 0.0)
                pick32[q * cs : (q + 1) * cs, :] = hit
            found = nt(both, pick32[...].astype(BF)) * weight
            col_at[...] = jnp.sum(found, axis=0, keepdims=True) - 1.0
            place_cols[c] = jnp.where(spots == col_at[...], 1.0, 0.0).astype(BF)

        each(0, nr, one)

    def settle(kk):
        for j in range(2):
            each(1, nr, lambda d: row_copy(2 * kk + j, d, row, row_from(row, d)).wait_recv())
        yy = pair_of(col, 2 * kk) // 2

        def widen(c):
            values = xrecv[c, pl.ds(2 * yy, 2)].reshape(4 * rs, nc * cs)
            full = nt(values, place_cols[c]).astype(BF).reshape(4, rs, fc)
            wide[:, pl.ds(pl.multiple_of(c * rs, 16), rs), :] = full

        each(0, nr, widen)
        ahead = lax.broadcasted_iota(i32, (256, nr * rs), 0)

        def rows_of_asm(i):
            rows = pl.ds(pl.multiple_of(i * 256, 256), 256)
            spots = (ahead + i * 256).astype(F32)
            for j in range(4):
                hit = jnp.where(spots == row_at[pl.ds(4 * yy + j, 1), :], 1.0, 0.0)
                place_rows[:, j * nr * rs : (j + 1) * nr * rs] = hit.astype(BF)
            asm[rows, :] += jnp.dot(
                place_rows[...], wide[...].reshape(4 * nr * rs, fc), preferred_element_type=F32)

        each(0, fr // 256, rows_of_asm)

    pc = fr // nc
    vc = pinv.shape[0] // nr

    def rows_of(ref, index, size):
        return ref.at[pl.ds(pl.multiple_of(index * size, size), size)]

    def pivot_out(d):
        return pltpu.make_async_remote_copy(
            rows_of(top16, d, vc), rows_of(pivot, d, vc), ss1.at[d], rs1.at[0],
            device_id={"row": d}, device_id_type=mesh)

    def panel_out(d):
        return pltpu.make_async_remote_copy(
            rows_of(asm16, d, pc), chunk, ss2.at[d], rs2.at[0],
            device_id={"col": d}, device_id_type=mesh)

    def pivot_share(d, whose):
        part = rows_of(pivot, whose, vc)
        return pltpu.make_async_remote_copy(
            part, part, ss3.at[d], rs3.at[d],
            device_id={"row": row_peer(row, d)}, device_id_type=mesh)

    def panel_share(d, whose):
        part = rows_of(panel, whose, pc)
        return pltpu.make_async_remote_copy(
            part, part, ss4.at[d], rs4.at[d],
            device_id={"col": col_peer(col, d)}, device_id_type=mesh)

    def load(i, src, dst):
        return pltpu.make_async_copy(src, dst, loads.at[i])

    load(0, child_in, child).start()
    load(1, parent_in, parent).start()
    load(2, pinv_in, pinv).start()
    lbuf[pl.ds(pl.multiple_of(col * width, width), width), :] = left[...]
    greet(nr, nc, row, col)
    for h in range(2):
        go(h, 0, (0, 0), None, (1, 0))
        go(h, 1, (0, 0), None, (-1, 0))
    for h in range(2):
        spread(h, 0)

    before = lax.broadcasted_iota(i32, (width, width), 0) < lax.broadcasted_iota(i32, (width, width), 1)
    tri[...] = jnp.where(before, 1.0, 0.0).astype(BF)
    own = maps[pl.ds(row, 1), pl.ds(pl.multiple_of(col * width, width), width)] // fc
    mask[0:nc, :] = jnp.where(own == lax.broadcasted_iota(i32, (nc, width), 0), 1.0, 0.0)
    ranks(nc, slots)
    steps_c = lax.broadcasted_iota(i32, (cs, width), 0).astype(F32)
    for g in range(nc):
        pick32[g * cs : (g + 1) * cs, :] = jnp.where(slots[g : g + 1, :] == steps_c, 1.0, 0.0)
    pick_cols[...] = pick32[...].astype(BF)
    mixing = jnp.dot(core[...], right[...], preferred_element_type=F32).astype(BF)
    pick(steps, mixing)
    each(1, nc, lambda d: mix_copy(d, col_peer(col, d), col).start())
    load(0, child_in, child).wait()
    each(0, steps, lambda t: pick(
        t, child[pl.ds(pl.multiple_of(t * 2 * width, 2 * width), 2 * width), :]))
    issue(0)
    for h in range(2):
        arrived(h, 0, (-1, 0), None)
        go(h, 2, (-1, 0), 0, (1, 0))
        arrived(h, 1, (1, 0), None)
        go(h, 3, (1, 0), 1, (-1, 0))
    for h in range(2):
        spread(h, 1)
        spread(h, 2)
    for h in range(2):
        onward(h, 0)
    issue(1)

    groups = lax.broadcasted_iota(i32, (nr, width), 0)
    for b in range(nb):
        there = maps[pl.ds(row, 1), b * width : (b + 1) * width] // fr
        mask[b * nr : (b + 1) * nr, :] = jnp.where(there == groups, 1.0, 0.0)
    ranks(nb * nr, slots)
    each(1, nc, lambda d: mix_copy(d, col, col_from(col, d)).wait_recv())
    low, high = parts(steps)
    msel[:, :width] = low.astype(BF)
    msel[:, width:] = high.astype(BF)

    forward(0)
    for h in range(2):
        arrived(h, 2, (-2, 0), 0)
        arrived(h, 3, (2, 0), 1)
        spread(h, 3)
    for h in range(2):
        last(h, 0)
        onward(h, 1)
        onward(h, 2)
    issue(2)
    issue(3)
    forward(1)
    for h in range(2):
        onward(h, 3)
    for h in range(2):
        last(h, 1)
        last(h, 2)
    issue(4)
    issue(5)
    forward(2)
    for h in range(2):
        last(h, 3)
    issue(6)
    issue(7)
    far_rows()
    forward(3)
    far_cols()
    forward(4)
    load(1, parent_in, parent).wait()
    load(2, pinv_in, pinv).wait()
    asm[...] = parent[...].astype(F32)
    forward(5)
    settle(0)
    forward(6)
    forward(7)
    each(1, 4, settle)

    @pl.when(col == 0)
    def _():
        asm16[...] = asm[...].astype(BF)
        each(1, nc, lambda d: panel_out(d).start())
        chunk[...] = asm16[0:pc, :]

    @pl.when(row == 0)
    def _():
        top16[...] = asm[0 : vc * nr, :].astype(BF)
        each(1, nr, lambda d: pivot_out(d).start())
        pivot[0:vc, :] = top16[0:vc, :]

    @pl.when(row > 0)
    def _():
        pivot_out(row).wait_recv()

    each(1, nr, lambda d: pivot_share(d, row).start())

    @pl.when(col > 0)
    def _():
        panel_out(col).wait_recv()

    part = jnp.dot(chunk[...].astype(F32), pinv[...], precision=HI, preferred_element_type=F32)
    panel[pl.ds(pl.multiple_of(col * pc, pc), pc), :] = part.astype(BF)
    each(1, nc, lambda d: panel_share(d, col).start())

    @pl.when(col == 0)
    def _():
        def rows_panel(i):
            rows = pl.ds(pl.multiple_of(i * 256, 256), 256)
            own_panel[rows, :] = jnp.dot(
                asm[rows, :], pinv[...], precision=HI, preferred_element_type=F32)

        each(0, fr // 256, rows_panel)

    def sent_all(k):
        each(1, nr, lambda d: row_copy(k, d, row_peer(row, d), row).wait_send())
        each(1, nc, lambda d: col_copy(k, d, col_peer(col, d), col).wait_send())

    each(0, steps, sent_all)
    each(1, nc, lambda d: mix_copy(d, col_peer(col, d), col).wait_send())
    for copy in sent:
        copy.wait_send()
    each(1, nr, lambda d: pivot_share(d, row_from(row, d)).wait_recv())
    each(1, nc, lambda d: panel_share(d, col_from(col, d)).wait_recv())
    each(1, nr, lambda d: pivot_share(d, row).wait_send())
    each(1, nc, lambda d: panel_share(d, col).wait_send())

    @pl.when(col == 0)
    def _():
        each(1, nc, lambda d: panel_out(d).wait_send())

    @pl.when(row == 0)
    def _():
        each(1, nr, lambda d: pivot_out(d).wait_send())


def front_parts(nr, nc, cs, rs, left, child, core, right, maps, parent, pinv):
    order, width = child.shape
    rank = left.shape[1]
    fr, fc = parent.shape
    pw = pinv.shape[0]
    nb = order // width
    vmem = pl.BlockSpec(memory_space=pltpu.VMEM)
    anywhere = pl.BlockSpec(memory_space=pl.ANY)
    dma = pltpu.SemaphoreType.DMA
    scratch = pltpu.VMEM
    return pl.pallas_call(
        lambda *refs: front_kernel(nr, nc, fr, fc, cs, rs, *refs),
        out_shape=(
            jax.ShapeDtypeStruct((fr, fc), F32),
            jax.ShapeDtypeStruct((fr, pw), BF),
            jax.ShapeDtypeStruct((pw, fc), BF),
            jax.ShapeDtypeStruct((fr, pw), F32),
        ),
        in_specs=[vmem, anywhere, vmem, vmem, vmem, anywhere, anywhere],
        out_specs=(vmem, vmem, vmem, vmem),
        scratch_shapes=[
            scratch((order, width), BF),
            scratch((fr, fc), BF),
            scratch((pw, pw), F32),
            scratch((order, rank), BF),
            scratch((nc * cs, rank), BF),
            scratch((nc * cs, 2 * width), F32),
            scratch((width, width), BF),
            scratch((nb * nr, width), F32),
            scratch((nb * nr, width), F32),
            scratch((nb * nr, width), F32),
            scratch((nb, 2 * nr, width), BF),
            scratch((nr * rs, width), BF),
            scratch((nc * cs, width), F32),
            scratch((nc * cs, width), BF),
            scratch((2, nr * rs, width), BF),
            scratch((nb, nr * rs), F32),
            scratch((1, nc * cs), F32),
            scratch((nr, fc, nc * cs), BF),
            scratch((256, 4 * nr * rs), BF),
            scratch((4, nr * rs, fc), BF),
            scratch((nb // 2 + 1, nc, 2 * cs, width), BF),
            scratch((nb // 2 + 1, nc, 2 * cs, width), BF),
            scratch((nb // 2, nr, 2 * rs, nc * cs), BF),
            scratch((nr, nb // 2, 2 * rs, nc * cs), BF),
            scratch((fr, fc), BF),
            scratch((pw, fc), BF),
            scratch((fr // nc, fc), BF),
            dma((2, 20)), dma((2, 20)),
            dma((nb // 2 + 1, nc)), dma((nb // 2 + 1, nc)),
            dma((nb // 2, nr)), dma((nb // 2, nr)),
            dma((nr,)), dma((1,)), dma((nc,)), dma((1,)),
            dma((nr,)), dma((nr,)), dma((nc,)), dma((nc,)),
            dma((3,)),
        ],
        compiler_params=pltpu.CompilerParams(
            collective_id=0, has_side_effects=True, vmem_limit_bytes=60 * 1024 * 1024
        ),
        name="front_parts",
    )(left, child, core, right, maps, parent, pinv)


def on_device(
    child_block, left_gen, core_gen, right_gen, child_maps, parent_entries, pivot_inverse
):
    nr = lax.axis_size("row")
    nc = lax.axis_size("col")
    row_me = lax.axis_index("row")
    col_me = lax.axis_index("col")
    order = child_block.shape[1]
    fr, fc = parent_entries.shape
    unit = order // (16 * nr * nr)
    cs = 6 * unit
    rs = 12 * unit
    pw = pivot_inverse.shape[0]
    assembled, panel_rows, pivot, local_panel = front_parts(
        nr, nc, cs, rs, left_gen[0], child_block[0], core_gen[0], right_gen[0], child_maps,
        parent_entries, pivot_inverse,
    )
    trailing = assembled - jnp.dot(panel_rows, pivot, preferred_element_type=F32)
    global_rows = row_me * fr + jnp.arange(fr, dtype=jnp.int32)
    lower = jnp.where(col_me == 0, local_panel, trailing)
    return jnp.where(global_rows[:, None] < pw, assembled, lower)


def solution(mesh):
    return jax.shard_map(
        on_device,
        mesh=mesh,
        in_specs=(
            P("row", None, "col"),
            P("row", "col", None),
            P("row", None, None),
            P("row", None, "col"),
            P(),
            P("row", "col"),
            P(),
        ),
        out_specs=P("row", "col"),
        check_vma=False,
    )
```

```python
import jax
import jax.numpy as jnp
from jax import lax
from jax.experimental import pallas as pl
from jax.experimental.pallas import tpu as pltpu
from jax.sharding import PartitionSpec as P

BF = jnp.bfloat16
F32 = jnp.float32
HI = lax.Precision.HIGHEST


def col_peer(me, d):
    y = lax.rem(me // 4 + d // 4, 4)
    z = lax.rem(lax.rem(me, 4) + lax.rem(d, 4), 4)
    return y * 4 + z


def row_peer(me, d):
    x = lax.rem(me // 2 + d // 2, 4)
    core = lax.rem(lax.rem(me, 2) + lax.rem(d, 2), 2)
    return x * 2 + core


def col_from(me, d):
    y = lax.rem(me // 4 + 4 - d // 4, 4)
    z = lax.rem(lax.rem(me, 4) + 4 - lax.rem(d, 4), 4)
    return y * 4 + z


def row_from(me, d):
    x = lax.rem(me // 2 + 4 - d // 2, 4)
    core = lax.rem(lax.rem(me, 2) + lax.rem(d, 2), 2)
    return x * 2 + core


def each(low, high, body):
    def step(i, carry):
        body(i)
        return carry

    lax.fori_loop(low, high, step, 0)


def greet(nr, nc, row, col):
    barrier = pltpu.get_barrier_semaphore()
    each(1, nc, lambda d: pl.semaphore_signal(
        barrier, inc=1, device_id={"col": col_peer(col, d)}, device_id_type=pl.DeviceIdType.MESH))
    each(1, nr, lambda d: pl.semaphore_signal(
        barrier, inc=1, device_id={"row": row_peer(row, d)}, device_id_type=pl.DeviceIdType.MESH))
    return lambda: pl.semaphore_wait(barrier, nc + nr - 2)


def nt(a, b):
    return lax.dot_general(a, b, (((1,), (1,)), ((), ())), preferred_element_type=F32)


def front_kernel(
    nr, nc, fr, fc, cs, rs,
    left, child_in, core, right, maps, parent_in, pinv_in,
    front,
    asm, panel, pivot, solved,
    child, parent, pinv, lbuf, msel, product, tri, mask, slots, far_slots, digits, sel,
    pick32, pick_cols, pick_rows, row_at, col_at, place_cols, place_rows, wide,
    zsend, zrecv, xsend, xrecv, asm16, top16,
    ls, lr, zs, zr, xs, xr, ss1, rs1, ss2, rs2, ss3, rs3, ss4, rs4, loads, stores,
):
    row = lax.axis_index("row")
    col = lax.axis_index("col")
    mesh = pl.DeviceIdType.MESH
    i32 = jnp.int32
    width = child.shape[1]
    nb = child.shape[0] // width
    half, quarter = width // 2, width // 4
    steps = nb // 2
    y, z = col // 4, lax.rem(col, 4)

    def at(dy, dz):
        return lax.rem(y + dy + 4, 4) * 4 + lax.rem(z + dz + 4, 4)

    def off(h, p, s):
        return at(s, p) if h == 0 else at(p, s)

    def piece(h, block, part):
        size = half if part is None else quarter
        start = h * half + (0 if part is None else part * quarter)
        return pl.ds(pl.multiple_of(block * width + start, quarter), size)

    def hop(h, m, src_off, part, to):
        where = piece(h, off(h, *src_off), part)
        return pltpu.make_async_remote_copy(
            lbuf.at[where], lbuf.at[where], ls.at[h, m], lr.at[h, m],
            device_id={"col": off(h, *to)}, device_id_type=mesh)

    def arrived(h, m, src_off, part):
        where = piece(h, off(h, *src_off), part)
        pltpu.make_async_remote_copy(
            lbuf.at[where], lbuf.at[where], ls.at[h, m], lr.at[h, m],
            device_id={"col": col}, device_id_type=mesh).wait_recv()

    sent = []

    def go(h, m, src_off, part, to):
        copy = hop(h, m, src_off, part, to)
        copy.start()
        sent.append(copy)

    ks = (0, -1, 1, 2)

    def spread(h, n):
        go(h, 4 + 4 * n, (ks[n], 0), None, (0, 1))
        go(h, 5 + 4 * n, (ks[n], 0), None, (0, -1))

    def onward(h, n):
        arrived(h, 4 + 4 * n, (ks[n], -1), None)
        go(h, 6 + 4 * n, (ks[n], -1), 0, (0, 1))
        arrived(h, 5 + 4 * n, (ks[n], 1), None)
        go(h, 7 + 4 * n, (ks[n], 1), 1, (0, -1))

    def last(h, n):
        arrived(h, 6 + 4 * n, (ks[n], -2), 0)
        arrived(h, 7 + 4 * n, (ks[n], 2), 1)

    def pair_of(who, k):
        kk = k // 2
        dy = kk + kk // 2 - 2 * (kk // 3)
        return lax.rem(who // 4 + dy, 4) * 2 + lax.rem(lax.rem(who, 4) // 2 + lax.rem(k, 2), 2)

    def col_copy(k, d, to, whose):
        t = pair_of(to, k)
        return pltpu.make_async_remote_copy(
            zsend.at[t, to], zrecv.at[t, whose], zs.at[k, d], zr.at[k, d],
            device_id={"col": to}, device_id_type=mesh)

    def mix_copy(d, to, whose):
        return pltpu.make_async_remote_copy(
            zsend.at[steps, to], zrecv.at[steps, whose], zs.at[steps, d], zr.at[steps, d],
            device_id={"col": to}, device_id_type=mesh)

    def issue(k):
        each(1, nc, lambda d: col_copy(k, d, col_peer(col, d), col).start())

    def pick(t, rows):
        picked = nt(pick_cols[...], rows).reshape(nc, cs // 8, 8, 2 * width)
        low = picked[:, :, None, :, :width]
        high = picked[:, :, None, :, width:]
        both = jnp.concatenate([low, high], axis=2).reshape(nc, 2 * cs, width)
        zsend[t] = both.astype(BF)
        zrecv[t, col] = zsend[t, col]

    def parts(t):
        got = zrecv[t].astype(F32).reshape(nc, cs // 8, 2, 8, width)
        return [got[:, :, h].reshape(nc * cs, width) for h in range(2)]

    def ranks(rows, into):
        counted = jnp.dot(mask[0:rows, :].astype(BF), tri[...], preferred_element_type=F32)
        into[0:rows, :] = jnp.where(mask[0:rows, :] > 0.5, counted, -1.0)

    steps_r = lax.broadcasted_iota(i32, (rs, width), 0).astype(F32)

    def row_copy(k, d, to, whose):
        t = pair_of(col, k)
        return pltpu.make_async_remote_copy(
            xsend.at[t, to], xrecv.at[whose, t], xs.at[k, d], xr.at[k, d],
            device_id={"row": to}, device_id_type=mesh)

    def forward(k):
        t = pair_of(col, k)
        for h in range(2):
            eight = slots[pl.ds(pl.multiple_of((2 * t + h) * nr, nr), nr), :]
            for g in range(nr):
                hit = jnp.where(eight[g : g + 1, :] == steps_r, 1.0, 0.0)
                pick_rows[h, g * rs : (g + 1) * rs, :] = hit.astype(BF)
        rows = pl.ds(pl.multiple_of(t * 2 * width, 2 * width), 2 * width)
        product[...] = nt(msel[...], lbuf[rows, :])
        each(1, nc, lambda d: col_copy(k, d, col, col_from(col, d)).wait_recv())
        got = parts(t)
        for h in range(2):
            update = (got[h] - product[:, h * width : (h + 1) * width]).astype(BF)
            chosen = nt(pick_rows[h], update)
            xsend[t, :, h * rs : (h + 1) * rs, :] = chosen.reshape(nr, rs, nc * cs).astype(BF)
        xrecv[row, t] = xsend[t, row]
        each(1, nr, lambda d: row_copy(k, d, row_peer(row, d), row).start())

    def split(targets):
        high = targets // 32
        return high.astype(F32), (targets - high * 32).astype(F32)

    def far_rows():
        for b in range(nb):
            here = maps[:, b * width : (b + 1) * width]
            mask[b * nr : (b + 1) * nr, :] = jnp.where(here // fr == row, 1.0, 0.0)
            high, low = split(here - row * fr + 1)
            digits[b] = jnp.concatenate([high, low], axis=0).astype(BF)
        ranks(nb * nr, far_slots)
        size = nr * rs
        sub = lax.broadcasted_iota(i32, (2 * nr, size), 0)
        lane = lax.broadcasted_iota(i32, (2 * nr, size), 1)
        weight = jnp.where(lane // rs == lax.rem(sub, nr), jnp.where(sub < nr, 32.0, 1.0), 0.0)

        def one(b):
            eight = far_slots[pl.ds(pl.multiple_of(b * nr, nr), nr), :]
            for g in range(nr):
                hit = jnp.where(eight[g : g + 1, :] == steps_r, 1.0, 0.0)
                sel[g * rs : (g + 1) * rs, :] = hit.astype(BF)
            found = nt(digits[b], sel[...]) * weight
            row_at[pl.ds(b, 1), :] = jnp.sum(found, axis=0, keepdims=True) - 1.0

        each(0, nb, one)

    def far_cols():
        size = nc * cs
        sub = lax.broadcasted_iota(i32, (2 * nc, size), 0)
        lane = lax.broadcasted_iota(i32, (2 * nc, size), 1)
        weight = jnp.where(lane // cs == lax.rem(sub, nc), jnp.where(sub < nc, 32.0, 1.0), 0.0)
        spots = lax.broadcasted_iota(i32, (fc, size), 0).astype(F32)

        def one(c):
            for q in range(nc):
                here = maps[pl.ds(c, 1), q * width : (q + 1) * width]
                mask[q : q + 1, :] = jnp.where(here // fc == col, 1.0, 0.0)
                high, low = split(here - col * fc + 1)
                pick32[q : q + 1, :] = high
                pick32[nc + q : nc + q + 1, :] = low
            both = pick32[0 : 2 * nc, :].astype(BF)
            ranks(nc, far_slots)
            for q in range(nc):
                hit = jnp.where(far_slots[q : q + 1, :] == steps_c, 1.0, 0.0)
                pick32[q * cs : (q + 1) * cs, :] = hit
            found = nt(both, pick32[...].astype(BF)) * weight
            col_at[...] = jnp.sum(found, axis=0, keepdims=True) - 1.0
            place_cols[c] = jnp.where(spots == col_at[...], 1.0, 0.0).astype(BF)

        each(0, nr, one)

    def settle(kk):
        for j in range(2):
            each(1, nr, lambda d: row_copy(2 * kk + j, d, row, row_from(row, d)).wait_recv())
        yy = pair_of(col, 2 * kk) // 2

        def widen(c):
            values = xrecv[c, pl.ds(2 * yy, 2)].reshape(4 * rs, nc * cs)
            full = nt(values, place_cols[c]).astype(BF).reshape(4, rs, fc)
            wide[:, pl.ds(pl.multiple_of(c * rs, 16), rs), :] = full

        each(0, nr, widen)
        ahead = lax.broadcasted_iota(i32, (256, nr * rs), 0)

        def rows_of_asm(i):
            rows = pl.ds(pl.multiple_of(i * 256, 256), 256)
            spots = (ahead + i * 256).astype(F32)
            for j in range(4):
                hit = jnp.where(spots == row_at[pl.ds(4 * yy + j, 1), :], 1.0, 0.0)
                place_rows[:, j * nr * rs : (j + 1) * nr * rs] = hit.astype(BF)
            asm[rows, :] += jnp.dot(
                place_rows[...], wide[...].reshape(4 * nr * rs, fc), preferred_element_type=F32)

        each(0, fr // 256, rows_of_asm)

    pc = fr // nc
    vc = pinv.shape[0] // nr

    def rows_of(ref, index, size):
        return ref.at[pl.ds(pl.multiple_of(index * size, size), size)]

    def pivot_out(d):
        return pltpu.make_async_remote_copy(
            rows_of(top16, d, vc), rows_of(pivot, d, vc), ss1.at[d], rs1.at[0],
            device_id={"row": d}, device_id_type=mesh)

    def half_of(h, index):
        return pl.ds(pl.multiple_of(index * pc + h * (pc // 2), pc // 2), pc // 2)

    def panel_out(h, d):
        return pltpu.make_async_remote_copy(
            asm16.at[half_of(h, d)], panel.at[half_of(h, d)], ss2.at[h, d], rs2.at[h],
            device_id={"col": d}, device_id_type=mesh)

    def pivot_share(d, whose):
        part = rows_of(pivot, whose, vc)
        return pltpu.make_async_remote_copy(
            part, part, ss3.at[d], rs3.at[d],
            device_id={"row": row_peer(row, d)}, device_id_type=mesh)

    def panel_share(h, d, whose):
        part = panel.at[half_of(h, whose)]
        return pltpu.make_async_remote_copy(
            part, part, ss4.at[h, d], rs4.at[h, d],
            device_id={"col": col_peer(col, d)}, device_id_type=mesh)

    def store(i):
        rows = pl.ds(pl.multiple_of(i * 256, 256), 256)
        return pltpu.make_async_copy(asm.at[rows], front.at[rows], stores.at[i])

    def load(i, src, dst):
        return pltpu.make_async_copy(src, dst, loads.at[i])

    load(0, child_in, child).start()
    load(1, parent_in, parent).start()
    load(2, pinv_in, pinv).start()
    lbuf[pl.ds(pl.multiple_of(col * width, width), width), :] = left[...]
    greeted = greet(nr, nc, row, col)
    before = lax.broadcasted_iota(i32, (width, width), 0) < lax.broadcasted_iota(i32, (width, width), 1)
    tri[...] = jnp.where(before, 1.0, 0.0).astype(BF)
    own = maps[pl.ds(row, 1), pl.ds(pl.multiple_of(col * width, width), width)] // fc
    mask[0:nc, :] = jnp.where(own == lax.broadcasted_iota(i32, (nc, width), 0), 1.0, 0.0)
    ranks(nc, slots)
    steps_c = lax.broadcasted_iota(i32, (cs, width), 0).astype(F32)
    for g in range(nc):
        pick32[g * cs : (g + 1) * cs, :] = jnp.where(slots[g : g + 1, :] == steps_c, 1.0, 0.0)
    pick_cols[...] = pick32[...].astype(BF)
    greeted()
    for h in range(2):
        go(h, 0, (0, 0), None, (1, 0))
        go(h, 1, (0, 0), None, (-1, 0))
    for h in range(2):
        spread(h, 0)

    mixing = jnp.dot(core[...], right[...], preferred_element_type=F32).astype(BF)
    pick(steps, mixing)
    each(1, nc, lambda d: mix_copy(d, col_peer(col, d), col).start())
    load(0, child_in, child).wait()

    def pick_and_send(i):
        t = lax.rem(pair_of(col, 0) + i, steps)
        pick(t, child[pl.ds(pl.multiple_of(t * 2 * width, 2 * width), 2 * width), :])
        for j in range(2):
            ty, tz = t // 2, lax.rem(t, 2) * 2 + j
            to = ty * 4 + tz

            @pl.when(to != col)
            def _():
                col_copy(0, lax.rem(ty - y + 4, 4) * 4 + lax.rem(tz - z + 4, 4), to, col).start()

    each(0, steps, pick_and_send)
    for h in range(2):
        arrived(h, 0, (-1, 0), None)
        go(h, 2, (-1, 0), 0, (1, 0))
        arrived(h, 1, (1, 0), None)
        go(h, 3, (1, 0), 1, (-1, 0))
    for h in range(2):
        spread(h, 1)
        spread(h, 2)
    for h in range(2):
        onward(h, 0)

    groups = lax.broadcasted_iota(i32, (nr, width), 0)
    for b in range(nb):
        there = maps[pl.ds(row, 1), b * width : (b + 1) * width] // fr
        mask[b * nr : (b + 1) * nr, :] = jnp.where(there == groups, 1.0, 0.0)
    ranks(nb * nr, slots)
    each(1, nc, lambda d: mix_copy(d, col, col_from(col, d)).wait_recv())
    low, high = parts(steps)
    msel[:, :width] = low.astype(BF)
    msel[:, width:] = high.astype(BF)

    forward(0)
    for h in range(2):
        arrived(h, 2, (-2, 0), 0)
        arrived(h, 3, (2, 0), 1)
        spread(h, 3)
    for h in range(2):
        last(h, 0)
        onward(h, 1)
        onward(h, 2)
    issue(1)
    issue(2)
    forward(1)
    for h in range(2):
        onward(h, 3)
    for h in range(2):
        last(h, 1)
        last(h, 2)
    issue(3)
    issue(4)
    forward(2)
    for h in range(2):
        last(h, 3)
    issue(5)
    far_rows()
    forward(3)
    issue(6)
    far_cols()
    forward(4)
    issue(7)
    load(1, parent_in, parent).wait()
    load(2, pinv_in, pinv).wait()
    asm[...] = parent[...].astype(F32)
    forward(5)
    settle(0)
    forward(6)
    settle(1)
    forward(7)
    each(2, 4, settle)

    @pl.when(col == 0)
    def _():
        asm16[...] = asm[...].astype(BF)
        for h in range(2):
            each(1, nc, lambda d: panel_out(h, d).start())
        panel[0:pc, :] = asm16[0:pc, :]

    @pl.when(row == 0)
    def _():
        top16[...] = asm[0 : vc * nr, :].astype(BF)
        each(1, nr, lambda d: pivot_out(d).start())
        pivot[0:vc, :] = top16[0:vc, :]

    @pl.when(row > 0)
    def _():
        pivot_out(row).wait_recv()

    each(1, nr, lambda d: pivot_share(d, row).start())
    for h in range(2):

        @pl.when(col > 0)
        def _():
            panel_out(h, col).wait_recv()

        each(1, nc, lambda d: panel_share(h, d, col).start())

    def sent_all(k):
        each(1, nr, lambda d: row_copy(k, d, row_peer(row, d), row).wait_send())
        each(1, nc, lambda d: col_copy(k, d, col_peer(col, d), col).wait_send())

    each(0, steps, sent_all)
    each(1, nc, lambda d: mix_copy(d, col_peer(col, d), col).wait_send())
    for copy in sent:
        copy.wait_send()
    each(1, nr, lambda d: pivot_share(d, row_from(row, d)).wait_recv())
    solved[...] = jnp.dot(
        pinv[...], pivot[...].astype(F32), precision=HI, preferred_element_type=F32).astype(BF)

    def close(dy):
        def arrive(dz):
            d = dy * 4 + dz
            for h in range(2):
                panel_share(h, d, col_from(col, d)).wait_recv()

        each(jnp.where(dy == 0, 1, 0), 4, arrive)
        i = lax.rem(y + 4 - dy, 4)
        rows = pl.ds(pl.multiple_of(i * 256, 256), 256)
        lower = jnp.logical_or(row > 0, i >= vc * nr // 256)

        @pl.when(jnp.logical_and(lower, col > 0))
        def _():
            asm[rows, :] -= jnp.dot(panel[rows, :], solved[...], preferred_element_type=F32)

        @pl.when(jnp.logical_and(lower, col == 0))
        def _():
            asm[rows, :] = jnp.dot(
                asm[rows, :], pinv[...], precision=HI, preferred_element_type=F32)

        store(i).start()

    each(0, 4, close)
    each(1, nr, lambda d: pivot_share(d, row).wait_send())
    for h in range(2):
        each(1, nc, lambda d: panel_share(h, d, col).wait_send())

    @pl.when(col == 0)
    def _():
        for h in range(2):
            each(1, nc, lambda d: panel_out(h, d).wait_send())

    @pl.when(row == 0)
    def _():
        each(1, nr, lambda d: pivot_out(d).wait_send())

    each(0, 4, lambda i: store(i).wait())


def front_parts(nr, nc, cs, rs, left, child, core, right, maps, parent, pinv):
    order, width = child.shape
    rank = left.shape[1]
    fr, fc = parent.shape
    pw = pinv.shape[0]
    nb = order // width
    vmem = pl.BlockSpec(memory_space=pltpu.VMEM)
    anywhere = pl.BlockSpec(memory_space=pl.ANY)
    dma = pltpu.SemaphoreType.DMA
    scratch = pltpu.VMEM
    return pl.pallas_call(
        lambda *refs: front_kernel(nr, nc, fr, fc, cs, rs, *refs),
        out_shape=jax.ShapeDtypeStruct((fr, fc), F32),
        in_specs=[vmem, anywhere, vmem, vmem, vmem, anywhere, anywhere],
        out_specs=anywhere,
        scratch_shapes=[
            scratch((fr, fc), F32),
            scratch((fr, pw), BF),
            scratch((pw, fc), BF),
            scratch((pw, fc), BF),
            scratch((order, width), BF),
            scratch((fr, fc), BF),
            scratch((pw, pw), F32),
            scratch((order, rank), BF),
            scratch((nc * cs, rank), BF),
            scratch((nc * cs, 2 * width), F32),
            scratch((width, width), BF),
            scratch((nb * nr, width), F32),
            scratch((nb * nr, width), F32),
            scratch((nb * nr, width), F32),
            scratch((nb, 2 * nr, width), BF),
            scratch((nr * rs, width), BF),
            scratch((nc * cs, width), F32),
            scratch((nc * cs, width), BF),
            scratch((2, nr * rs, width), BF),
            scratch((nb, nr * rs), F32),
            scratch((1, nc * cs), F32),
            scratch((nr, fc, nc * cs), BF),
            scratch((256, 4 * nr * rs), BF),
            scratch((4, nr * rs, fc), BF),
            scratch((nb // 2 + 1, nc, 2 * cs, width), BF),
            scratch((nb // 2 + 1, nc, 2 * cs, width), BF),
            scratch((nb // 2, nr, 2 * rs, nc * cs), BF),
            scratch((nr, nb // 2, 2 * rs, nc * cs), BF),
            scratch((fr, fc), BF),
            scratch((pw, fc), BF),
            dma((2, 20)), dma((2, 20)),
            dma((nb // 2 + 1, nc)), dma((nb // 2 + 1, nc)),
            dma((nb // 2, nr)), dma((nb // 2, nr)),
            dma((nr,)), dma((1,)), dma((2, nc)), dma((2,)),
            dma((nr,)), dma((nr,)), dma((2, nc)), dma((2, nc)),
            dma((3,)), dma((4,)),
        ],
        compiler_params=pltpu.CompilerParams(
            collective_id=0, has_side_effects=True, vmem_limit_bytes=60 * 1024 * 1024
        ),
        name="front_parts",
    )(left, child, core, right, maps, parent, pinv)


def on_device(
    child_block, left_gen, core_gen, right_gen, child_maps, parent_entries, pivot_inverse
):
    nr = lax.axis_size("row")
    nc = lax.axis_size("col")
    order = child_block.shape[1]
    unit = order // (16 * nr * nr)
    cs = 6 * unit
    rs = 12 * unit
    return front_parts(
        nr, nc, cs, rs, left_gen[0], child_block[0], core_gen[0], right_gen[0], child_maps,
        parent_entries, pivot_inverse,
    )


def solution(mesh):
    return jax.shard_map(
        on_device,
        mesh=mesh,
        in_specs=(
            P("row", None, "col"),
            P("row", "col", None),
            P("row", None, None),
            P("row", None, "col"),
            P(),
            P("row", "col"),
            P(),
        ),
        out_specs=P("row", "col"),
        check_vma=False,
    )
```

```python
import jax
import jax.numpy as jnp
from jax import lax
from jax.experimental import pallas as pl
from jax.experimental.pallas import tpu as pltpu
from jax.sharding import PartitionSpec as P

BF = jnp.bfloat16
F32 = jnp.float32


def col_peer(me, d):
    y = lax.rem(me // 4 + d // 4, 4)
    z = lax.rem(lax.rem(me, 4) + lax.rem(d, 4), 4)
    return y * 4 + z


def row_peer(me, d):
    x = lax.rem(me // 2 + d // 2, 4)
    core = lax.rem(lax.rem(me, 2) + lax.rem(d, 2), 2)
    return x * 2 + core


def col_from(me, d):
    y = lax.rem(me // 4 + 4 - d // 4, 4)
    z = lax.rem(lax.rem(me, 4) + 4 - lax.rem(d, 4), 4)
    return y * 4 + z


def row_from(me, d):
    x = lax.rem(me // 2 + 4 - d // 2, 4)
    core = lax.rem(lax.rem(me, 2) + lax.rem(d, 2), 2)
    return x * 2 + core


def each(low, high, body):
    def step(i, carry):
        body(i)
        return carry

    lax.fori_loop(low, high, step, 0)


def greet(nr, nc, row, col):
    barrier = pltpu.get_barrier_semaphore()
    each(1, nc, lambda d: pl.semaphore_signal(
        barrier, inc=1, device_id={"col": col_peer(col, d)}, device_id_type=pl.DeviceIdType.MESH))
    each(1, nr, lambda d: pl.semaphore_signal(
        barrier, inc=1, device_id={"row": row_peer(row, d)}, device_id_type=pl.DeviceIdType.MESH))
    return lambda: pl.semaphore_wait(barrier, nc + nr - 2)


def nt(a, b):
    return lax.dot_general(a, b, (((1,), (1,)), ((), ())), preferred_element_type=F32)


def front_kernel(
    nr, nc, fr, fc, cs, rs,
    left, child_in, core, right, maps, parent_in, pinv_in,
    front,
    asm, panel, pivot, solved, pin_high, pin_low,
    child, parent, pinv, lbuf, msel, product, tri, mask, slots, far_slots, digits, sel,
    pick32, pick_cols, pick_rows, row_at, col_at, place_cols, place_rows, wide,
    zsend, zrecv, xsend, xrecv, asm16, top16,
    ls, lr, zs, zr, xs, xr, ss1, rs1, ss2, rs2, ss3, rs3, ss4, rs4, loads, stores,
):
    row = lax.axis_index("row")
    col = lax.axis_index("col")
    mesh = pl.DeviceIdType.MESH
    i32 = jnp.int32
    width = child.shape[1]
    nb = child.shape[0] // width
    half, quarter = width // 2, width // 4
    steps = nb // 2
    y, z = col // 4, lax.rem(col, 4)

    def at(dy, dz):
        return lax.rem(y + dy + 4, 4) * 4 + lax.rem(z + dz + 4, 4)

    def off(h, p, s):
        return at(s, p) if h == 0 else at(p, s)

    def piece(h, block, part):
        size = half if part is None else quarter
        start = h * half + (0 if part is None else part * quarter)
        return pl.ds(pl.multiple_of(block * width + start, quarter), size)

    def hop(h, m, src_off, part, to):
        where = piece(h, off(h, *src_off), part)
        return pltpu.make_async_remote_copy(
            lbuf.at[where], lbuf.at[where], ls.at[h, m], lr.at[h, m],
            device_id={"col": off(h, *to)}, device_id_type=mesh)

    def arrived(h, m, src_off, part):
        where = piece(h, off(h, *src_off), part)
        pltpu.make_async_remote_copy(
            lbuf.at[where], lbuf.at[where], ls.at[h, m], lr.at[h, m],
            device_id={"col": col}, device_id_type=mesh).wait_recv()

    sent = []

    def go(h, m, src_off, part, to):
        copy = hop(h, m, src_off, part, to)
        copy.start()
        sent.append(copy)

    ks = (0, -1, 1, 2)

    def spread(h, n):
        go(h, 4 + 4 * n, (ks[n], 0), None, (0, 1))
        go(h, 5 + 4 * n, (ks[n], 0), None, (0, -1))

    def onward(h, n):
        arrived(h, 4 + 4 * n, (ks[n], -1), None)
        go(h, 6 + 4 * n, (ks[n], -1), 0, (0, 1))
        arrived(h, 5 + 4 * n, (ks[n], 1), None)
        go(h, 7 + 4 * n, (ks[n], 1), 1, (0, -1))

    def last(h, n):
        arrived(h, 6 + 4 * n, (ks[n], -2), 0)
        arrived(h, 7 + 4 * n, (ks[n], 2), 1)

    def pair_of(who, k):
        kk = k // 2
        dy = kk + kk // 2 - 2 * (kk // 3)
        return lax.rem(who // 4 + dy, 4) * 2 + lax.rem(lax.rem(who, 4) // 2 + lax.rem(k, 2), 2)

    def col_copy(k, d, to, whose):
        t = pair_of(to, k)
        return pltpu.make_async_remote_copy(
            zsend.at[t, to], zrecv.at[t, whose], zs.at[k, d], zr.at[k, d],
            device_id={"col": to}, device_id_type=mesh)

    def mix_copy(d, to, whose):
        return pltpu.make_async_remote_copy(
            zsend.at[steps, to], zrecv.at[steps, whose], zs.at[steps, d], zr.at[steps, d],
            device_id={"col": to}, device_id_type=mesh)

    def issue(k):
        each(1, nc, lambda d: col_copy(k, d, col_peer(col, d), col).start())

    def pick(t, rows):
        picked = nt(pick_cols[...], rows).reshape(nc, cs // 8, 8, 2 * width)
        low = picked[:, :, None, :, :width]
        high = picked[:, :, None, :, width:]
        both = jnp.concatenate([low, high], axis=2).reshape(nc, 2 * cs, width)
        zsend[t] = both.astype(BF)
        zrecv[t, col] = zsend[t, col]

    def parts(t):
        got = zrecv[t].astype(F32).reshape(nc, cs // 8, 2, 8, width)
        return [got[:, :, h].reshape(nc * cs, width) for h in range(2)]

    def ranks(rows, into):
        counted = jnp.dot(mask[0:rows, :].astype(BF), tri[...], preferred_element_type=F32)
        into[0:rows, :] = jnp.where(mask[0:rows, :] > 0.5, counted, -1.0)

    steps_r = lax.broadcasted_iota(i32, (rs, width), 0).astype(F32)

    def row_copy(k, d, to, whose):
        t = pair_of(col, k)
        return pltpu.make_async_remote_copy(
            xsend.at[t, to], xrecv.at[whose, t], xs.at[k, d], xr.at[k, d],
            device_id={"row": to}, device_id_type=mesh)

    def forward(k):
        t = pair_of(col, k)
        for h in range(2):
            eight = slots[pl.ds(pl.multiple_of((2 * t + h) * nr, nr), nr), :]
            for g in range(nr):
                hit = jnp.where(eight[g : g + 1, :] == steps_r, 1.0, 0.0)
                pick_rows[h, g * rs : (g + 1) * rs, :] = hit.astype(BF)
        rows = pl.ds(pl.multiple_of(t * 2 * width, 2 * width), 2 * width)
        product[...] = nt(msel[...], lbuf[rows, :])
        each(1, nc, lambda d: col_copy(k, d, col, col_from(col, d)).wait_recv())
        got = parts(t)
        for h in range(2):
            update = (got[h] - product[:, h * width : (h + 1) * width]).astype(BF)
            chosen = nt(pick_rows[h], update)
            xsend[t, :, h * rs : (h + 1) * rs, :] = chosen.reshape(nr, rs, nc * cs).astype(BF)
        xrecv[row, t] = xsend[t, row]
        each(1, nr, lambda d: row_copy(k, d, row_peer(row, d), row).start())

    def split(targets):
        high = targets // 32
        return high.astype(F32), (targets - high * 32).astype(F32)

    def far_rows():
        for b in range(nb):
            here = maps[:, b * width : (b + 1) * width]
            mask[b * nr : (b + 1) * nr, :] = jnp.where(here // fr == row, 1.0, 0.0)
            high, low = split(here - row * fr + 1)
            digits[b] = jnp.concatenate([high, low], axis=0).astype(BF)
        ranks(nb * nr, far_slots)
        size = nr * rs
        sub = lax.broadcasted_iota(i32, (2 * nr, size), 0)
        lane = lax.broadcasted_iota(i32, (2 * nr, size), 1)
        weight = jnp.where(lane // rs == lax.rem(sub, nr), jnp.where(sub < nr, 32.0, 1.0), 0.0)

        def one(b):
            eight = far_slots[pl.ds(pl.multiple_of(b * nr, nr), nr), :]
            for g in range(nr):
                hit = jnp.where(eight[g : g + 1, :] == steps_r, 1.0, 0.0)
                sel[g * rs : (g + 1) * rs, :] = hit.astype(BF)
            found = nt(digits[b], sel[...]) * weight
            row_at[pl.ds(b, 1), :] = jnp.sum(found, axis=0, keepdims=True) - 1.0

        each(0, nb, one)

    def far_cols():
        size = nc * cs
        sub = lax.broadcasted_iota(i32, (2 * nc, size), 0)
        lane = lax.broadcasted_iota(i32, (2 * nc, size), 1)
        weight = jnp.where(lane // cs == lax.rem(sub, nc), jnp.where(sub < nc, 32.0, 1.0), 0.0)
        spots = lax.broadcasted_iota(i32, (fc, size), 0).astype(F32)

        def one(c):
            for q in range(nc):
                here = maps[pl.ds(c, 1), q * width : (q + 1) * width]
                mask[q : q + 1, :] = jnp.where(here // fc == col, 1.0, 0.0)
                high, low = split(here - col * fc + 1)
                pick32[q : q + 1, :] = high
                pick32[nc + q : nc + q + 1, :] = low
            both = pick32[0 : 2 * nc, :].astype(BF)
            ranks(nc, far_slots)
            for q in range(nc):
                hit = jnp.where(far_slots[q : q + 1, :] == steps_c, 1.0, 0.0)
                pick32[q * cs : (q + 1) * cs, :] = hit
            found = nt(both, pick32[...].astype(BF)) * weight
            col_at[...] = jnp.sum(found, axis=0, keepdims=True) - 1.0
            place_cols[c] = jnp.where(spots == col_at[...], 1.0, 0.0).astype(BF)

        each(0, nr, one)

    pc = fr // nc
    vc = pinv.shape[0] // nr

    def rows_of(ref, index, size):
        return ref.at[pl.ds(pl.multiple_of(index * size, size), size)]

    def pivot_out(d):
        return pltpu.make_async_remote_copy(
            rows_of(top16, d, vc), rows_of(pivot, d, vc), ss1.at[d], rs1.at[0],
            device_id={"row": d}, device_id_type=mesh)

    def half_of(h, index):
        return pl.ds(pl.multiple_of(index * pc + h * (pc // 2), pc // 2), pc // 2)

    def panel_out(h, d):
        return pltpu.make_async_remote_copy(
            asm16.at[half_of(h, d)], panel.at[half_of(h, d)], ss2.at[h, d], rs2.at[h],
            device_id={"col": d}, device_id_type=mesh)

    def pivot_share(d, whose):
        part = rows_of(pivot, whose, vc)
        return pltpu.make_async_remote_copy(
            part, part, ss3.at[d], rs3.at[d],
            device_id={"row": row_peer(row, d)}, device_id_type=mesh)

    def panel_share(h, d, whose):
        part = panel.at[half_of(h, whose)]
        return pltpu.make_async_remote_copy(
            part, part, ss4.at[h, d], rs4.at[h, d],
            device_id={"col": col_peer(col, d)}, device_id_type=mesh)

    def store(i):
        rows = pl.ds(pl.multiple_of(i * 256, 256), 256)
        return pltpu.make_async_copy(asm.at[rows], front.at[rows], stores.at[i])

    def settle(kk, last):
        yy = pair_of(col, 2 * kk) // 2
        ahead = lax.broadcasted_iota(i32, (256, nr * rs), 0)

        def spots_of(i):
            rows = pl.ds(pl.multiple_of(i * 256, 256), 256)
            spots = (ahead + i * 256).astype(F32)
            for j in range(4):
                hit = jnp.where(spots == row_at[pl.ds(4 * yy + j, 1), :], 1.0, 0.0)
                place_rows[rows, j * nr * rs : (j + 1) * nr * rs] = hit.astype(BF)

        each(0, fr // 256, spots_of)
        for j in range(2):
            each(1, nr, lambda d: row_copy(2 * kk + j, d, row, row_from(row, d)).wait_recv())

        def widen(c):
            values = xrecv[c, pl.ds(2 * yy, 2)].reshape(4 * rs, nc * cs)
            full = nt(values, place_cols[c]).astype(BF).reshape(4, rs, fc)
            wide[:, pl.ds(pl.multiple_of(c * rs, 16), rs), :] = full

        each(0, nr, widen)

        def rows_of_asm(i):
            rows = pl.ds(pl.multiple_of(i * 256, 256), 256)
            asm[rows, :] += jnp.dot(
                place_rows[rows, :], wide[...].reshape(4 * nr * rs, fc), preferred_element_type=F32)
            if last:
                scatter(i, rows)

        each(0, fr // 256, rows_of_asm)

    def scatter(i, rows):
        first = jnp.where(i == 0, 1, 0)

        @pl.when(col == 0)
        def _():
            asm16[rows, :] = asm[rows, :].astype(BF)
            for h in range(2):
                each(first, 256 // pc, lambda j: panel_out(h, i * (256 // pc) + j).start())

        @pl.when(jnp.logical_and(row == 0, i < vc * nr // 256))
        def _():
            top16[rows, :] = asm[rows, :].astype(BF)
            each(first, 256 // vc, lambda j: pivot_out(i * (256 // vc) + j).start())

    def load(i, src, dst):
        return pltpu.make_async_copy(src, dst, loads.at[i])

    load(0, child_in, child).start()
    load(1, parent_in, parent).start()
    load(2, pinv_in, pinv).start()
    lbuf[pl.ds(pl.multiple_of(col * width, width), width), :] = left[...]
    greeted = greet(nr, nc, row, col)
    before = lax.broadcasted_iota(i32, (width, width), 0) < lax.broadcasted_iota(i32, (width, width), 1)
    tri[...] = jnp.where(before, 1.0, 0.0).astype(BF)
    own = maps[pl.ds(row, 1), pl.ds(pl.multiple_of(col * width, width), width)] // fc
    mask[0:nc, :] = jnp.where(own == lax.broadcasted_iota(i32, (nc, width), 0), 1.0, 0.0)
    ranks(nc, slots)
    steps_c = lax.broadcasted_iota(i32, (cs, width), 0).astype(F32)
    for g in range(nc):
        pick32[g * cs : (g + 1) * cs, :] = jnp.where(slots[g : g + 1, :] == steps_c, 1.0, 0.0)
    pick_cols[...] = pick32[...].astype(BF)
    greeted()
    for h in range(2):
        go(h, 0, (0, 0), None, (1, 0))
        go(h, 1, (0, 0), None, (-1, 0))
    for h in range(2):
        spread(h, 0)

    mixing = jnp.dot(core[...], right[...], preferred_element_type=F32).astype(BF)
    pick(steps, mixing)
    each(1, nc, lambda d: mix_copy(d, col_peer(col, d), col).start())
    load(0, child_in, child).wait()

    def pick_and_send(i):
        t = lax.rem(pair_of(col, 0) + i, steps)
        pick(t, child[pl.ds(pl.multiple_of(t * 2 * width, 2 * width), 2 * width), :])
        for j in range(2):
            ty, tz = t // 2, lax.rem(t, 2) * 2 + j
            to = ty * 4 + tz

            @pl.when(to != col)
            def _():
                col_copy(0, lax.rem(ty - y + 4, 4) * 4 + lax.rem(tz - z + 4, 4), to, col).start()

    each(0, steps, pick_and_send)
    for h in range(2):
        arrived(h, 0, (-1, 0), None)
        go(h, 2, (-1, 0), 0, (1, 0))
        arrived(h, 1, (1, 0), None)
        go(h, 3, (1, 0), 1, (-1, 0))
    for h in range(2):
        spread(h, 1)
        spread(h, 2)
    for h in range(2):
        onward(h, 0)

    groups = lax.broadcasted_iota(i32, (nr, width), 0)
    for b in range(nb):
        there = maps[pl.ds(row, 1), b * width : (b + 1) * width] // fr
        mask[b * nr : (b + 1) * nr, :] = jnp.where(there == groups, 1.0, 0.0)
    ranks(nb * nr, slots)
    each(1, nc, lambda d: mix_copy(d, col, col_from(col, d)).wait_recv())
    low, high = parts(steps)
    msel[:, :width] = low.astype(BF)
    msel[:, width:] = high.astype(BF)

    issue(1)
    forward(0)
    for h in range(2):
        arrived(h, 2, (-2, 0), 0)
        arrived(h, 3, (2, 0), 1)
        spread(h, 3)
    for h in range(2):
        last(h, 0)
        onward(h, 1)
        onward(h, 2)
    issue(2)
    forward(1)
    for h in range(2):
        onward(h, 3)
    for h in range(2):
        last(h, 1)
        last(h, 2)
    issue(3)
    issue(4)
    forward(2)
    for h in range(2):
        last(h, 3)
    issue(5)
    far_rows()
    forward(3)
    issue(6)
    far_cols()
    forward(4)
    issue(7)
    load(1, parent_in, parent).wait()
    load(2, pinv_in, pinv).wait()
    pin_high[...] = pinv[...].astype(BF)
    pin_low[...] = (pinv[...] - pin_high[...].astype(F32)).astype(BF)
    asm[...] = parent[...].astype(F32)
    forward(5)
    settle(0, False)
    forward(6)
    settle(1, False)
    forward(7)
    settle(2, False)
    settle(3, True)

    @pl.when(col == 0)
    def _():
        panel[0:pc, :] = asm16[0:pc, :]

    @pl.when(row == 0)
    def _():
        pivot[0:vc, :] = top16[0:vc, :]

    @pl.when(row > 0)
    def _():
        pivot_out(row).wait_recv()

    each(1, nr, lambda d: pivot_share(d, row).start())
    for h in range(2):

        @pl.when(col > 0)
        def _():
            panel_out(h, col).wait_recv()

        each(1, nc, lambda d: panel_share(h, d, col).start())

    def sent_all(k):
        each(1, nr, lambda d: row_copy(k, d, row_peer(row, d), row).wait_send())
        each(1, nc, lambda d: col_copy(k, d, col_peer(col, d), col).wait_send())

    each(0, steps, sent_all)
    each(1, nc, lambda d: mix_copy(d, col_peer(col, d), col).wait_send())
    for copy in sent:
        copy.wait_send()
    each(1, nr, lambda d: pivot_share(d, row_from(row, d)).wait_recv())
    solved[...] = (
        jnp.dot(pin_high[...], pivot[...], preferred_element_type=F32)
        + jnp.dot(pin_low[...], pivot[...], preferred_element_type=F32)).astype(BF)

    def close(dy):
        def arrive(dz):
            d = dy * 4 + dz
            for h in range(2):
                panel_share(h, d, col_from(col, d)).wait_recv()

        i = lax.rem(y + 4 - dy, 4)
        rows = pl.ds(pl.multiple_of(i * 256, 256), 256)
        lower = jnp.logical_or(row > 0, i >= vc * nr // 256)

        @pl.when(jnp.logical_and(lower, col == 0))
        def _():
            high = asm[rows, :].astype(BF)
            low = (asm[rows, :] - high.astype(F32)).astype(BF)
            asm[rows, :] = jnp.dot(high, pin_high[...], preferred_element_type=F32) + (
                jnp.dot(high, pin_low[...], preferred_element_type=F32)
                + jnp.dot(low, pin_high[...], preferred_element_type=F32))

        each(jnp.where(dy == 0, 1, 0), 4, arrive)

        @pl.when(jnp.logical_and(lower, col > 0))
        def _():
            asm[rows, :] -= jnp.dot(panel[rows, :], solved[...], preferred_element_type=F32)

        store(i).start()

    each(0, 4, close)
    each(1, nr, lambda d: pivot_share(d, row).wait_send())
    for h in range(2):
        each(1, nc, lambda d: panel_share(h, d, col).wait_send())

    @pl.when(col == 0)
    def _():
        for h in range(2):
            each(1, nc, lambda d: panel_out(h, d).wait_send())

    @pl.when(row == 0)
    def _():
        each(1, nr, lambda d: pivot_out(d).wait_send())

    each(0, 4, lambda i: store(i).wait())


def front_parts(nr, nc, cs, rs, left, child, core, right, maps, parent, pinv):
    order, width = child.shape
    rank = left.shape[1]
    fr, fc = parent.shape
    pw = pinv.shape[0]
    nb = order // width
    vmem = pl.BlockSpec(memory_space=pltpu.VMEM)
    anywhere = pl.BlockSpec(memory_space=pl.ANY)
    dma = pltpu.SemaphoreType.DMA
    scratch = pltpu.VMEM
    return pl.pallas_call(
        lambda *refs: front_kernel(nr, nc, fr, fc, cs, rs, *refs),
        out_shape=jax.ShapeDtypeStruct((fr, fc), F32),
        in_specs=[vmem, anywhere, vmem, vmem, vmem, anywhere, anywhere],
        out_specs=anywhere,
        scratch_shapes=[
            scratch((fr, fc), F32),
            scratch((fr, pw), BF),
            scratch((pw, fc), BF),
            scratch((pw, fc), BF),
            scratch((pw, pw), BF),
            scratch((pw, pw), BF),
            scratch((order, width), BF),
            scratch((fr, fc), BF),
            scratch((pw, pw), F32),
            scratch((order, rank), BF),
            scratch((nc * cs, rank), BF),
            scratch((nc * cs, 2 * width), F32),
            scratch((width, width), BF),
            scratch((nb * nr, width), F32),
            scratch((nb * nr, width), F32),
            scratch((nb * nr, width), F32),
            scratch((nb, 2 * nr, width), BF),
            scratch((nr * rs, width), BF),
            scratch((nc * cs, width), F32),
            scratch((nc * cs, width), BF),
            scratch((2, nr * rs, width), BF),
            scratch((nb, nr * rs), F32),
            scratch((1, nc * cs), F32),
            scratch((nr, fc, nc * cs), BF),
            scratch((fr, 4 * nr * rs), BF),
            scratch((4, nr * rs, fc), BF),
            scratch((nb // 2 + 1, nc, 2 * cs, width), BF),
            scratch((nb // 2 + 1, nc, 2 * cs, width), BF),
            scratch((nb // 2, nr, 2 * rs, nc * cs), BF),
            scratch((nr, nb // 2, 2 * rs, nc * cs), BF),
            scratch((fr, fc), BF),
            scratch((pw, fc), BF),
            dma((2, 20)), dma((2, 20)),
            dma((nb // 2 + 1, nc)), dma((nb // 2 + 1, nc)),
            dma((nb // 2, nr)), dma((nb // 2, nr)),
            dma((nr,)), dma((1,)), dma((2, nc)), dma((2,)),
            dma((nr,)), dma((nr,)), dma((2, nc)), dma((2, nc)),
            dma((3,)), dma((4,)),
        ],
        compiler_params=pltpu.CompilerParams(
            collective_id=0, has_side_effects=True, vmem_limit_bytes=60 * 1024 * 1024
        ),
        name="front_parts",
    )(left, child, core, right, maps, parent, pinv)


def on_device(
    child_block, left_gen, core_gen, right_gen, child_maps, parent_entries, pivot_inverse
):
    nr = lax.axis_size("row")
    nc = lax.axis_size("col")
    order = child_block.shape[1]
    unit = order // (16 * nr * nr)
    cs = 6 * unit
    rs = 12 * unit
    return front_parts(
        nr, nc, cs, rs, left_gen[0], child_block[0], core_gen[0], right_gen[0], child_maps,
        parent_entries, pivot_inverse,
    )


def solution(mesh):
    return jax.shard_map(
        on_device,
        mesh=mesh,
        in_specs=(
            P("row", None, "col"),
            P("row", "col", None),
            P("row", None, None),
            P("row", None, "col"),
            P(),
            P("row", "col"),
            P(),
        ),
        out_specs=P("row", "col"),
        check_vma=False,
    )
```
